256 devices in a mesh: rep: 64 (over z, x, core), shard: 4 (over y).
Axes of the slice: x: 4, y: 4, z: 8, core: 2. Of those that a mesh axis runs over, the one named last changes fastest.
Arguments:
- inputs: bfloat16 [20480, 4096], P('rep', 'shard'), may hold values from -6 to 6
- weight: float32 [4096, 4096], P('shard', 'rep'), may hold values from -0.09375 to 0.09375
- table: bfloat16 [256, 4096], replicated, may hold values from -6 to 6
- targets: int32 [20480], P(('rep', 'shard')), may hold values from 0 to 255
Outputs:
- combined: float32 [4096, 4096], P('shard', 'rep')
- new_weight: float32 [4096, 4096], P('shard', 'rep')
The draws below stay inside these ranges and needn't reach their ends.
All inputs are finite; a program needn't handle non-finite values.
Results may differ from the reference program's by a relative error of at most 0.005.
Values may be sent and summed in bfloat16 or wider, within the bound.
A program may use at most 128 MiB of HBM per device.

```python
import math
import jax
import jax.numpy as jnp
import numpy as np
from jax import lax

D = 4096
NBEST = 256
ROWS = 320
ALL_ROWS = 20480
N_REP = 64


def place_ends(array, rng, low, top_value):
    longest = array.shape.index(max(array.shape))
    spots = []
    for shift in (0, 1):
        where = [jax.random.randint(jax.random.fold_in(rng, axis), (), 0, length) for axis, length in enumerate(array.shape)]
        where[longest] = (where[longest] + shift) % array.shape[longest]
        spots.append(tuple(where))
    return array.at[spots[0]].set(low).at[spots[1]].set(top_value)


def level_of(rng, shape, pieces, low, top_value):
    level = 1.0
    for position, shards_of in pieces:
        draws = jax.random.uniform(jax.random.fold_in(jax.random.fold_in(rng, 6), position), (shards_of,), jnp.float32, low / len(pieces), top_value / len(pieces))
        level = level * jnp.repeat(jnp.exp(draws), shape[position] // shards_of).reshape((-1,) + (1,) * (len(shape) - 1 - position))
    return level


def rank_table(amount, lean):
    loads = [(1 << 20) // math.isqrt(grade ** lean) + 1 for grade in range(1, amount + 1)]
    spread = 1 + sum(loads) // (1 << 30)
    return np.cumsum(np.array([max(1, weight // spread) for weight in loads]))


def ranked_ids(stream_key, dims, count, slope):
    table = rank_table(count, slope)
    pick = jax.random.randint(jax.random.fold_in(stream_key, 1), dims, 0, int(table[count - 1]))
    rank = jnp.searchsorted(jnp.asarray(table, jnp.int32), pick, side="right")
    return jax.random.permutation(jax.random.fold_in(stream_key, 2), count)[rank].astype(jnp.int32)


def normal_values(key, extent, scale, bound, pieces=(), dtype=jnp.bfloat16):
    values = scale * jax.random.normal(key, extent, jnp.float32)
    if pieces:
        values = values * level_of(key, extent, pieces, -0.22, 0.18)
    return jnp.clip(values, -bound, bound).astype(dtype)


def setup_inputs(seed: int = 0) -> dict:
    streams_of = jax.random.split(jax.random.key(seed), 5)
    inputs = normal_values(streams_of[0], (ALL_ROWS, D), 1.0, 6.0, ((0, 64), (1, 4)))
    weight = normal_values(streams_of[1], (D, D), D ** -0.5, 0.09375, ((0, 4), (1, 64)), jnp.float32)
    table = normal_values(streams_of[2], (NBEST, D), 1.0, 6.0)
    targets = place_ends(ranked_ids(streams_of[3], (ALL_ROWS,), NBEST, 2), jax.random.fold_in(streams_of[3], 3), 0, NBEST - 1).astype(jnp.int32)
    return dict(inputs=inputs, weight=weight, table=table, targets=targets)


epsilon = 1e-06
step_size = 0.05

def adasum_pair(lower_vec, upper_vec):
    cross = jnp.sum(lower_vec * upper_vec)
    norm_low = jnp.sum(lower_vec * lower_vec)
    norm_high = jnp.sum(upper_vec * upper_vec)
    return (1.0 - cross / (2.0 * (norm_low + epsilon))) * lower_vec + (1.0 - cross / (2.0 * (norm_high + epsilon))) * upper_vec

def replica_grad(replica, inputs, weight_b, table, targets):
    row_block = inputs[replica * ROWS:(replica + 1) * ROWS].astype(jnp.float32)
    outputs = jnp.dot(row_block, weight_b, precision=lax.Precision.HIGHEST)
    wanted = table[targets[replica * ROWS:(replica + 1) * ROWS]].astype(jnp.float32)
    error = ((outputs - wanted) / ROWS).astype(jnp.bfloat16).astype(jnp.float32)
    return jnp.dot(row_block.T, error, precision=lax.Precision.HIGHEST)

def reference(inputs, weight, table, targets):
    weight_b = weight.astype(jnp.bfloat16).astype(jnp.float32)

    def subtree(low_end, high_end):
        if high_end - low_end == 1:
            return replica_grad(low_end, inputs, weight_b, table, targets)
        middle = (low_end + high_end) // 2
        return adasum_pair(subtree(low_end, middle), subtree(middle, high_end))
    combined = subtree(0, N_REP)
    return (combined, weight - step_size * combined)
```

```python
import functools

import jax
import jax.numpy as jnp
from jax import lax
from jax.experimental import pallas as pl
from jax.experimental.pallas import tpu as pltpu
from jax.sharding import Mesh
from jax.sharding import PartitionSpec as P

AXES = ("z", "x", "c", "shard")
REP = ("z", "x", "c")
MESH = pl.DeviceIdType.MESH
F32, BF16 = jnp.float32, jnp.bfloat16

EPS = 1e-06
STEP = 0.05

KX = (0, 0, -1, 1, -1, 1, 2, 2)
KC = (0, 1, 0, 0, 1, 1, 0, 1)
DZ = (0, -1, 1, -2, 2, -3, 3, 4)

ROWS, FEAT, PIECE, HALF = 320, 1024, 80, 256
UNITS = 16


def place_of(steps, other):
    return [i for i in range(8) if KX[i] % 4 == steps % 4 and KC[i] == other][0]


def block_of(steps):
    return [i for i in range(8) if DZ[i] % 8 == steps % 8][0]


def iotas(shape):
    return lax.broadcasted_iota(jnp.int32, shape, 0), lax.broadcasted_iota(jnp.int32, shape, 1)


def swap_bit(v, bit, axis):
    pos = lax.broadcasted_iota(jnp.int32, v.shape, axis)
    up = pltpu.roll(v, bit, axis)
    down = pltpu.roll(v, v.shape[axis] - bit, axis)
    return jnp.where((pos & bit) != 0, up, down)


def tree_coefficients(gram):
    sub, lane = iotas(gram.shape)
    coef = jnp.ones((8, 1), F32)
    for bit in (1, 2, 4):
        own = jnp.where(lane == sub, gram, 0.0)
        cross = jnp.where(lane == (sub ^ bit), gram, 0.0)

        def factor(axis):
            norm = jnp.maximum(jnp.sum(own, axis=axis, keepdims=True), 0.0)
            return 1.0 - jnp.sum(cross, axis=axis, keepdims=True) / (2.0 * (norm + EPS))

        by_row, by_col = factor(1), factor(0)
        coef = coef * by_row
        gram = gram * by_row * by_col
        gram = gram + swap_bit(gram, bit, 1)
        gram = gram + swap_bit(gram, bit, 0)
    return coef


def pick(coef, index):
    sub, _ = iotas((8, 1))
    return jnp.sum(jnp.where(sub == index, coef, 0.0), axis=0, keepdims=True)


def gram_matrix(sums, index_of):
    sub, lane = iotas((8, 128))
    gram = jnp.zeros((8, 128), F32)
    for a in range(8):
        for b in range(a + 1):
            v = jnp.sum(jnp.sum(sums[a, b], axis=0, keepdims=True), axis=1, keepdims=True)
            i, j = index_of(a), index_of(b)
            here = ((sub == i) & (lane == j)) | ((sub == j) & (lane == i))
            gram = jnp.where(here, v, gram)
    return gram


def kernel(
    x_ref, wt_ref, tgt_ref, table_ref, out_ref,
    X, W, TG, TB, TT, PF, S1, S2, R1, R2, E, G, GA, GB, CS, CB, OWN, AX, AY, AZ,
    loc_sem, w_s, w_r, x_s, x_r, t_s, t_r, y_s, y_r, c_s, c_r, a_s, a_r,
):
    z, x = lax.axis_index("z"), lax.axis_index("x")
    c, y = lax.axis_index("c"), lax.axis_index("shard")

    def zat(d):
        return {"z": lax.rem(z + (d % 8), 8)}

    def yat(d):
        return {"shard": lax.rem(y + (d % 4), 4)}

    def xcat(d, o):
        dev = {}
        if d % 4:
            dev["x"] = lax.rem(x + (d % 4), 4)
        if o:
            dev["c"] = 1 - c
        return dev

    def remote(src, dst, ssem, rsem, dev):
        return pltpu.make_async_remote_copy(
            src_ref=src, dst_ref=dst, send_sem=ssem, recv_sem=rsem, device_id=dev, device_id_type=MESH
        )

    own_x = pltpu.make_async_copy(x_ref, X.at[0], loc_sem.at[8])
    own_x.start()
    blocks = []
    for p in range(8):
        col = lax.rem(z + (DZ[p] % 8), 8) * 512 + x * 128
        cp = pltpu.make_async_copy(
            table_ref.at[:, pl.ds(pl.multiple_of(col, 128), 128)], TB.at[p], loc_sem.at[p]
        )
        cp.start()
        blocks.append(cp)

    barrier = pltpu.get_barrier_semaphore()
    others = [xcat(d, o) for d in range(4) for o in range(2) if d or o]
    others += [yat(d) for d in (1, 2, 3)]
    others += [zat(d) for d in range(1, 8)]
    for dev in others:
        pl.semaphore_signal(barrier, inc=1, device_id=dev, device_id_type=MESH)
    pl.semaphore_wait(barrier, len(others))

    def wslot(ref, d):
        p = block_of(d)
        return ref.at[p // 4, p % 4]

    def wcopy(i):
        n, sign = i // 2 + 1, (1 if i % 2 == 0 else -1)
        src = wt_ref if n == 1 else wslot(W, -sign * (n - 1))
        dst = wslot(W, -sign * n)
        if n == 4:
            rows = pl.ds(0, 32) if sign == 1 else pl.ds(32, 32)
            src, dst = src.at[rows], dst.at[rows]
        return remote(src, dst, w_s.at[i], w_r.at[i], zat(sign))

    wcopies = [wcopy(i) for i in range(8)]
    wcopies[0].start()
    wcopies[1].start()

    lo, hi = pl.ds(0, 160), pl.ds(160, 160)
    xc = [
        remote(X.at[0, lo], X.at[2, lo], x_s.at[0], x_r.at[0], xcat(1, 0)),
        remote(X.at[0, hi], X.at[3, hi], x_s.at[1], x_r.at[1], xcat(-1, 0)),
        remote(X.at[0], X.at[1], x_s.at[2], x_r.at[2], xcat(0, 1)),
        remote(X.at[0, hi], X.at[2, hi], x_s.at[3], x_r.at[3], xcat(1, 0)),
        remote(X.at[0, lo], X.at[3, lo], x_s.at[4], x_r.at[4], xcat(-1, 0)),
        remote(X.at[2, lo], X.at[6, lo], x_s.at[5], x_r.at[5], xcat(1, 0)),
        remote(X.at[3, hi], X.at[6, hi], x_s.at[6], x_r.at[6], xcat(-1, 0)),
        remote(X.at[2], X.at[4], x_s.at[7], x_r.at[7], xcat(0, 1)),
        remote(X.at[3], X.at[5], x_s.at[8], x_r.at[8], xcat(0, 1)),
        remote(X.at[6], X.at[7], x_s.at[9], x_r.at[9], xcat(0, 1)),
    ]
    own_x.wait()
    for i in range(5):
        xc[i].start()

    tcopies = []
    for k in range(1, 8):
        there = place_of(-KX[k], KC[k])
        tc = remote(tgt_ref, TG.at[there], t_s.at[k - 1], t_r.at[there - 1], xcat(KX[k], KC[k]))
        tc.start()
        tcopies.append(tc)
    TG[0] = tgt_ref[...]
    W[0, 0] = wt_ref[...]
    GA[...] = jnp.zeros_like(GA)

    for cp in blocks:
        cp.wait()
    _, lane = iotas((256, 128))
    for q in range(4):
        left = pltpu.roll(TB[2 * q].astype(F32), 64 * c, 1)
        right = pltpu.roll(TB[2 * q + 1].astype(F32), 64 * (1 - c), 1)
        TT[q // 2, :, (q % 2) * 128 : (q % 2) * 128 + 128] = jnp.where(lane < 64, left, right).astype(BF16)

    for tc in tcopies:
        tc.wait()

    for i in (0, 1):
        wcopies[i].wait_recv()
        wcopies[i + 2].start()
    for i in (2, 3):
        wcopies[i].wait_recv()
        wcopies[i + 2].start()

    yp, ym, y2 = lax.rem(y + 1, 4), lax.rem(y + 3, 4), lax.rem(y + 2, 4)

    def unit(u):
        early = u < 4
        k = jnp.where(early, lax.rem(u, 2), u // 2)
        h = jnp.where(early, u // 2, lax.rem(u, 2))
        return k, h

    def r1(u, d):
        return remote(S1.at[u, d], R1.at[u, d], y_s.at[0, d, u], y_r.at[0, d, u], yat(1 - 2 * d))

    def r2(u, d):
        return remote(S2.at[u, d], R2.at[u, d], y_s.at[1, d, u], y_r.at[1, d, u], yat(1 - 2 * d))

    def a1(u, d, who):
        k, h = unit(u)
        ref = E.at[k, h, who]
        return remote(ref, ref, y_s.at[2, d, u], y_r.at[2, d, u], yat(1 - 2 * d))

    def a2(u, d, who):
        k, h = unit(u)
        ref = E.at[k, h, who, :, pl.ds(128 * d, 128)]
        return remote(ref, ref, y_s.at[3, d, u], y_r.at[3, d, u], yat(1 - 2 * d))

    def forward(u):
        k, h = unit(u)
        slot = lax.rem(u, 4)

        @pl.when(u == 1)
        def _():
            xc[2].wait_recv()

        @pl.when(u == 2)
        def _():
            wcopies[6].wait_recv()
            wcopies[7].wait_recv()

        @pl.when(u == 4)
        def _():
            xc[3].wait_recv()
            xc[7].start()

        @pl.when(u == 6)
        def _():
            xc[4].wait_recv()
            xc[8].start()

        @pl.when(u == 8)
        def _():
            xc[7].wait_recv()

        @pl.when(u == 10)
        def _():
            xc[8].wait_recv()

        @pl.when(u == 12)
        def _():
            xc[5].wait_recv()
            xc[6].wait_recv()
            xc[9].start()

        @pl.when(u == 14)
        def _():
            xc[9].wait_recv()

        part = lax.dot_general(
            X[k], W[h].reshape(HALF, FEAT), (((1,), (1,)), ((), ())), preferred_element_type=F32
        )
        PF[slot] = part.reshape(4, PIECE, HALF)
        far = PF[slot, y2].astype(BF16)
        S1[u, 0] = far[:, :128]
        S1[u, 1] = far[:, 128:]
        r1(u, 0).start()
        r1(u, 1).start()
        row = TG[k][0:1]
        sub, _ = iotas((256, 128))
        one_hot = (sub == row).astype(F32).astype(BF16)
        wanted = lax.dot_general(one_hot, TT[h], (((0,), (0,)), ((), ())), preferred_element_type=F32)
        PF[slot, y] = PF[slot, y] - wanted[:PIECE]

        @pl.when(u == 0)
        def _():
            for i in (4, 5):
                wcopies[i].wait_recv()
                wcopies[i + 2].start()

        @pl.when(u == 1)
        def _():
            xc[0].wait_recv()
            xc[5].start()
            xc[1].wait_recv()
            xc[6].start()

    def reduce_step(u):
        slot = lax.rem(u, 4)
        r1(u, 0).wait_recv()
        r1(u, 1).wait_recv()
        S2[u, 0, :, :128] = (PF[slot, yp, :, :128] + R1[u, 0].astype(F32)).astype(BF16)
        S2[u, 0, :, 128:] = PF[slot, yp, :, 128:].astype(BF16)
        r2(u, 0).start()
        S2[u, 1, :, :128] = PF[slot, ym, :, :128].astype(BF16)
        S2[u, 1, :, 128:] = (PF[slot, ym, :, 128:] + R1[u, 1].astype(F32)).astype(BF16)
        r2(u, 1).start()

    def error_step(u):
        k, h = unit(u)
        slot = lax.rem(u, 4)
        r2(u, 0).wait_recv()
        r2(u, 1).wait_recv()
        total = PF[slot, y] + R2[u, 0].astype(F32) + R2[u, 1].astype(F32)
        E[k, h, y] = (total * (1.0 / ROWS)).astype(BF16)
        a1(u, 0, y).start()
        a1(u, 1, y).start()

    def spread_step(u):
        a1(u, 0, ym).wait_recv()
        a2(u, 0, ym).start()
        a1(u, 1, yp).wait_recv()
        a2(u, 1, yp).start()

    def grad_step(u):
        k, h = unit(u)
        a2(u, 0, y2).wait_recv()
        a2(u, 1, y2).wait_recv()
        err = E[k, h].reshape(ROWS, HALF)
        G[k, h] = lax.dot_general(err, X[k], (((0,), (0,)), ((), ())), preferred_element_type=F32)
        for kk in range(8):

            @pl.when(k == kk)
            def _():
                def block(i, sums):
                    rows = pl.ds(pl.multiple_of(i * 8, 8), 8)
                    sums = list(sums)
                    for j in range(FEAT // 128):
                        cols = pl.ds(j * 128, 128)
                        mine = G[kk, h, rows, cols]
                        for l in range(kk):
                            sums[l] = sums[l] + mine * G[l, h, rows, cols]
                        sums[kk] = sums[kk] + mine * mine
                    return tuple(sums)

                sums = lax.fori_loop(
                    0, HALF // 8, block, tuple(jnp.zeros((8, 128), F32) for _ in range(kk + 1))
                )
                for l in range(kk + 1):
                    GA[kk, l] += sums[l]

        for d in range(2):
            r1(u, d).wait_send()
            r2(u, d).wait_send()
            a1(u, d, y).wait_send()
            a2(u, d, ym if d == 0 else yp).wait_send()

    def turn(t, carry):
        @pl.when((t >= 3) & (t < UNITS + 3))
        def _():
            spread_step(t - 3)

        @pl.when((t >= 2) & (t < UNITS + 2))
        def _():
            error_step(t - 2)

        @pl.when((t >= 1) & (t < UNITS + 1))
        def _():
            reduce_step(t - 1)

        @pl.when(t < UNITS)
        def _():
            forward(t)

        @pl.when(t >= 4)
        def _():
            grad_step(t - 4)

        return carry

    lax.fori_loop(0, UNITS + 4, turn, 0)

    def sum_xc(value, s):
        AX[s, 0] = value
        copies = []
        for k in range(1, 8):
            there = place_of(-KX[k], KC[k])
            cp = remote(AX.at[s, 0], AX.at[s, there], a_s.at[s, k], a_r.at[s, there], xcat(KX[k], KC[k]))
            cp.start()
            copies.append(cp)
        for cp in copies:
            cp.wait()
        return functools.reduce(jnp.add, [AX[s, k] for k in range(8)])

    def sum_y(value, s):
        AY[s, 0] = value
        copies = []
        for d in range(1, 4):
            cp = remote(AY.at[s, 0], AY.at[s, 4 - d], a_s.at[2 + s, d], a_r.at[2 + s, 4 - d], yat(d))
            cp.start()
            copies.append(cp)
        for cp in copies:
            cp.wait()
        return functools.reduce(jnp.add, [AY[s, k] for k in range(4)])

    def sum_z(value):
        AZ[0] = value
        copies = []
        for d in range(1, 8):
            cp = remote(AZ.at[0], AZ.at[8 - d], a_s.at[4, d], a_r.at[4, 8 - d], zat(d))
            cp.start()
            copies.append(cp)
        for cp in copies:
            cp.wait()
        return functools.reduce(jnp.add, [AZ[k] for k in range(8)])

    def replica(k):
        return lax.rem(x + (KX[k] % 4), 4) * 2 + lax.rem(c + KC[k], 2)

    coef = tree_coefficients(sum_y(sum_xc(gram_matrix(GA, replica), 0), 0))
    weights = [pick(coef, replica(k)) for k in range(8)]

    ccopies = {}
    for p in (7, 5, 6, 3, 4, 1, 2, 0):

        def mix(i, carry):
            rows = pl.ds(pl.multiple_of((p % 4) * 64 + i * 16, 16), 16)
            total = weights[0] * G[0, p // 4, rows, :]
            for k in range(1, 8):
                total = total + weights[k] * G[k, p // 4, rows, :]
            here = pl.ds(pl.multiple_of(i * 16, 16), 16)
            if p == 0:
                OWN[here, :] = total
            else:
                CS[p, here, :] = total.astype(BF16)
            return carry

        lax.fori_loop(0, 4, mix, 0)
        if p:
            there = block_of(-DZ[p])
            ccopies[there] = remote(CS.at[p], CB.at[there], c_s.at[p], c_r.at[there], zat(DZ[p]))
            ccopies[there].start()

    for p in range(8):
        if p:
            ccopies[p].wait_recv()

        def block(i, sums, p=p):
            rows = pl.ds(pl.multiple_of(i * 16, 16), 16)
            sums = list(sums)
            for j in range(FEAT // 128):
                cols = pl.ds(j * 128, 128)

                def read(q):
                    return CB[q, rows, cols].astype(F32) if q else OWN[rows, cols]

                mine = read(p)
                for l in range(p + 1):
                    prod = mine * read(l)
                    sums[l] = sums[l] + prod[:8] + prod[8:]
            return tuple(sums)

        sums = lax.fori_loop(0, 4, block, tuple(jnp.zeros((8, 128), F32) for _ in range(p + 1)))
        for l in range(p + 1):
            GB[p, l] = sums[l]

    def plane(p):
        return lax.rem(z + (DZ[p] % 8), 8)

    coef = tree_coefficients(sum_z(sum_y(sum_xc(gram_matrix(GB, plane), 1), 1)))
    weights = [pick(coef, plane(p)) for p in range(8)]

    def final(i, carry):
        rows = pl.ds(pl.multiple_of(i * 16, 16), 16)
        total = weights[0] * OWN[rows, :]
        for p in range(1, 8):
            total = total + weights[p] * CB[p, rows, :].astype(F32)
        out_ref[rows, :] = total
        return carry

    lax.fori_loop(0, 4, final, 0)

    for cp in wcopies + xc + list(ccopies.values()):
        cp.wait_send()


def on_device(inputs, weight, table, targets):
    wt = weight.T.astype(BF16)
    tgt = jnp.broadcast_to(jnp.pad(targets, (0, 48))[None], (8, 128))
    vmem = pl.BlockSpec(memory_space=pltpu.VMEM)
    anywhere = pl.BlockSpec(memory_space=pl.ANY)
    dma = pltpu.SemaphoreType.DMA
    combined_t = pl.pallas_call(
        kernel,
        out_shape=jax.ShapeDtypeStruct((64, FEAT), F32),
        in_specs=[anywhere, vmem, vmem, anywhere],
        out_specs=vmem,
        scratch_shapes=[
            pltpu.VMEM((8, ROWS, FEAT), BF16),
            pltpu.VMEM((2, 4, 64, FEAT), BF16),
            pltpu.VMEM((8, 8, 128), jnp.int32),
            pltpu.VMEM((8, 256, 128), BF16),
            pltpu.VMEM((2, 256, HALF), BF16),
            pltpu.VMEM((4, 4, PIECE, HALF), F32),
            pltpu.VMEM((UNITS, 2, PIECE, 128), BF16),
            pltpu.VMEM((UNITS, 2, PIECE, HALF), BF16),
            pltpu.VMEM((UNITS, 2, PIECE, 128), BF16),
            pltpu.VMEM((UNITS, 2, PIECE, HALF), BF16),
            pltpu.VMEM((8, 2, 4, PIECE, HALF), BF16),
            pltpu.VMEM((8, 2, HALF, FEAT), F32),
            pltpu.VMEM((8, 8, 8, 128), F32),
            pltpu.VMEM((8, 8, 8, 128), F32),
            pltpu.VMEM((8, 64, FEAT), BF16),
            pltpu.VMEM((8, 64, FEAT), BF16),
            pltpu.VMEM((64, FEAT), F32),
            pltpu.VMEM((2, 8, 8, 128), F32),
            pltpu.VMEM((2, 4, 8, 128), F32),
            pltpu.VMEM((8, 8, 128), F32),
            dma((9,)),
            dma((8,)),
            dma((8,)),
            dma((10,)),
            dma((10,)),
            dma((7,)),
            dma((7,)),
            dma((4, 2, UNITS)),
            dma((4, 2, UNITS)),
            dma((8,)),
            dma((8,)),
            dma((5, 8)),
            dma((5, 8)),
        ],
        compiler_params=pltpu.CompilerParams(
            collective_id=0, has_side_effects=True, vmem_limit_bytes=56 * 1024 * 1024
        ),
    )(inputs, wt, tgt, table)
    combined = combined_t.T
    return combined, weight - STEP * combined


def solution(mesh):
    split = Mesh(mesh.devices.reshape(8, 4, 2, mesh.shape["shard"]), AXES)
    return jax.shard_map(
        on_device,
        mesh=split,
        in_specs=(P(REP, "shard"), P("shard", REP), P(), P(REP + ("shard",))),
        out_specs=(P("shard", REP), P("shard", REP)),
        check_vma=False,
    )
```

```python
import functools

import jax
import jax.numpy as jnp
from jax import lax
from jax.experimental import pallas as pl
from jax.experimental.pallas import tpu as pltpu
from jax.sharding import Mesh
from jax.sharding import PartitionSpec as P

AXES = ("z", "x", "c", "shard")
REP = ("z", "x", "c")
MESH = pl.DeviceIdType.MESH
F32, BF16 = jnp.float32, jnp.bfloat16

EPS = 1e-06
STEP = 0.05

KX = (0, 0, -1, 1, -1, 1, 2, 2)
KC = (0, 1, 0, 0, 1, 1, 0, 1)
DZ = (0, -1, 1, -2, 2, -3, 3, 4)

ROWS, FEAT, PIECE, HALF = 320, 1024, 80, 256
UNITS, LAG = 16, 2


def place_of(steps, other):
    return [i for i in range(8) if KX[i] % 4 == steps % 4 and KC[i] == other][0]


def block_of(steps):
    return [i for i in range(8) if DZ[i] % 8 == steps % 8][0]


def iotas(shape):
    return lax.broadcasted_iota(jnp.int32, shape, 0), lax.broadcasted_iota(jnp.int32, shape, 1)


def swap_bit(v, bit, axis):
    pos = lax.broadcasted_iota(jnp.int32, v.shape, axis)
    up = pltpu.roll(v, bit, axis)
    down = pltpu.roll(v, v.shape[axis] - bit, axis)
    return jnp.where((pos & bit) != 0, up, down)


def tree_coefficients(gram):
    sub, lane = iotas(gram.shape)
    coef = jnp.ones((8, 1), F32)
    for bit in (1, 2, 4):
        own = jnp.where(lane == sub, gram, 0.0)
        cross = jnp.where(lane == (sub ^ bit), gram, 0.0)

        def factor(axis):
            norm = jnp.maximum(jnp.sum(own, axis=axis, keepdims=True), 0.0)
            return 1.0 - jnp.sum(cross, axis=axis, keepdims=True) / (2.0 * (norm + EPS))

        by_row, by_col = factor(1), factor(0)
        coef = coef * by_row
        gram = gram * by_row * by_col
        gram = gram + swap_bit(gram, bit, 1)
        gram = gram + swap_bit(gram, bit, 0)
    return coef


def pick(coef, index):
    sub, _ = iotas((8, 1))
    return jnp.sum(jnp.where(sub == index, coef, 0.0), axis=0, keepdims=True)


def gram_matrix(sums, index_of):
    sub, lane = iotas((8, 128))
    gram = jnp.zeros((8, 128), F32)
    for a in range(8):
        for b in range(a + 1):
            v = jnp.sum(jnp.sum(sums[a, b], axis=0, keepdims=True), axis=1, keepdims=True)
            i, j = index_of(a), index_of(b)
            here = ((sub == i) & (lane == j)) | ((sub == j) & (lane == i))
            gram = jnp.where(here, v, gram)
    return gram


def kernel(
    x_ref, w_ref, tgt_ref, table_ref, out_ref,
    X, W, TG, TB, TT, PF, S1, S2, R1, R2, E, G, GA, GB, CS, CB, OWN, AX, AY, AZ,
    loc_sem, w_s, w_r, x_s, x_r, t_s, t_r, y_s, y_r, c_s, c_r, a_s, a_r,
):
    z, x = lax.axis_index("z"), lax.axis_index("x")
    c, y = lax.axis_index("c"), lax.axis_index("shard")

    def zat(d):
        return {"z": lax.rem(z + (d % 8), 8)}

    def yat(d):
        return {"shard": lax.rem(y + (d % 4), 4)}

    def xcat(d, o):
        dev = {}
        if d % 4:
            dev["x"] = lax.rem(x + (d % 4), 4)
        if o:
            dev["c"] = 1 - c
        return dev

    def remote(src, dst, ssem, rsem, dev):
        return pltpu.make_async_remote_copy(
            src_ref=src, dst_ref=dst, send_sem=ssem, recv_sem=rsem, device_id=dev, device_id_type=MESH
        )

    TG[0] = jnp.zeros((8, 128), jnp.int32)
    TG[0, 0:1, 0:PIECE] = tgt_ref[...]

    own_x = pltpu.make_async_copy(x_ref, X.at[0], loc_sem.at[8])
    own_x.start()
    blocks = []
    for p in range(8):
        col = lax.rem(z + (DZ[p] % 8), 8) * 512 + x * 128
        cp = pltpu.make_async_copy(
            table_ref.at[:, pl.ds(pl.multiple_of(col, 128), 128)], TB.at[p], loc_sem.at[p]
        )
        cp.start()
        blocks.append(cp)

    barrier = pltpu.get_barrier_semaphore()
    others = [xcat(d, o) for d in range(4) for o in range(2) if d or o]
    others += [yat(d) for d in (1, 2, 3)]
    others += [zat(d) for d in range(1, 8)]
    for dev in others:
        pl.semaphore_signal(barrier, inc=1, device_id=dev, device_id_type=MESH)
    pl.semaphore_wait(barrier, len(others))

    def wslot(d):
        p = block_of(d)
        return W.at[p // 4, p % 4]

    def wcopy(i):
        n, sign = i // 2 + 1, (1 if i % 2 == 0 else -1)
        src = wslot(0) if n <= 2 else wslot(-sign * 2)
        dst = wslot(-sign * n)
        if n == 4:
            rows = pl.ds(0, 32) if sign == 1 else pl.ds(32, 32)
            src, dst = src.at[rows], dst.at[rows]
        return remote(src, dst, w_s.at[i], w_r.at[i], zat(sign * (n if n <= 2 else n - 2)))

    W[0, 0] = w_ref[...].astype(BF16)
    wcopies = [wcopy(i) for i in range(8)]
    for i in range(4):
        wcopies[i].start()

    lo, hi = pl.ds(0, 160), pl.ds(160, 160)
    xc = [
        remote(X.at[0, lo], X.at[2, lo], x_s.at[0], x_r.at[0], xcat(1, 0)),
        remote(X.at[0, hi], X.at[3, hi], x_s.at[1], x_r.at[1], xcat(-1, 0)),
        remote(X.at[0], X.at[1], x_s.at[2], x_r.at[2], xcat(0, 1)),
        remote(X.at[0, hi], X.at[2, hi], x_s.at[3], x_r.at[3], xcat(1, 0)),
        remote(X.at[0, lo], X.at[3, lo], x_s.at[4], x_r.at[4], xcat(-1, 0)),
        remote(X.at[2, lo], X.at[6, lo], x_s.at[5], x_r.at[5], xcat(1, 0)),
        remote(X.at[3, hi], X.at[6, hi], x_s.at[6], x_r.at[6], xcat(-1, 0)),
        remote(X.at[2], X.at[4], x_s.at[7], x_r.at[7], xcat(0, 1)),
        remote(X.at[3], X.at[5], x_s.at[8], x_r.at[8], xcat(0, 1)),
        remote(X.at[6], X.at[7], x_s.at[9], x_r.at[9], xcat(0, 1)),
    ]
    own_x.wait()
    for i in range(5):
        xc[i].start()

    tcopies = []
    for k in range(1, 8):
        there = place_of(-KX[k], KC[k])
        tc = remote(TG.at[0], TG.at[there], t_s.at[k - 1], t_r.at[there - 1], xcat(KX[k], KC[k]))
        tc.start()
        tcopies.append(tc)
    GA[...] = jnp.zeros_like(GA)

    for cp in blocks:
        cp.wait()
    _, lane = iotas((256, 128))
    for q in range(4):
        left = pltpu.roll(TB[2 * q].astype(F32), 64 * c, 1)
        right = pltpu.roll(TB[2 * q + 1].astype(F32), 64 * (1 - c), 1)
        TT[q // 2, :, (q % 2) * 128 : (q % 2) * 128 + 128] = jnp.where(lane < 64, left, right).astype(BF16)

    for tc in tcopies:
        tc.wait()

    for i in (0, 1):
        wcopies[i].wait_recv()
    for i in (2, 3):
        wcopies[i].wait_recv()
        wcopies[i + 2].start()
        wcopies[i + 4].start()

    yp, ym, y2 = lax.rem(y + 1, 4), lax.rem(y + 3, 4), lax.rem(y + 2, 4)

    def unit(u):
        early = u < 4
        k = jnp.where(early, lax.rem(u, 2), u // 2)
        h = jnp.where(early, u // 2, lax.rem(u, 2))
        return k, h

    def r1(u, d):
        return remote(S1.at[u, d], R1.at[u, d], y_s.at[0, d, u], y_r.at[0, d, u], yat(1 - 2 * d))

    def r2(u, d):
        return remote(S2.at[u, d], R2.at[u, d], y_s.at[1, d, u], y_r.at[1, d, u], yat(1 - 2 * d))

    def a1(u, d, who):
        k, h = unit(u)
        ref = E.at[k, h, who]
        return remote(ref, ref, y_s.at[2, d, u], y_r.at[2, d, u], yat(1 - 2 * d))

    def a2(u, d, who):
        k, h = unit(u)
        ref = E.at[k, h, who, :, pl.ds(128 * d, 128)]
        return remote(ref, ref, y_s.at[3, d, u], y_r.at[3, d, u], yat(1 - 2 * d))

    def forward(u):
        k, h = unit(u)
        slot = lax.rem(u, 8)

        @pl.when(u == 1)
        def _():
            xc[2].wait_recv()

        @pl.when(u == 2)
        def _():
            for i in (4, 5, 6, 7):
                wcopies[i].wait_recv()

        @pl.when(u == 4)
        def _():
            xc[3].wait_recv()
            xc[7].start()

        @pl.when(u == 6)
        def _():
            xc[4].wait_recv()
            xc[8].start()

        @pl.when(u == 8)
        def _():
            xc[7].wait_recv()

        @pl.when(u == 10)
        def _():
            xc[8].wait_recv()

        @pl.when(u == 12)
        def _():
            xc[5].wait_recv()
            xc[6].wait_recv()
            xc[9].start()

        @pl.when(u == 14)
        def _():
            xc[9].wait_recv()

        part = lax.dot_general(
            X[k], W[h].reshape(HALF, FEAT), (((1,), (1,)), ((), ())), preferred_element_type=F32
        )
        PF[slot] = part.reshape(4, PIECE, HALF)
        far = PF[slot, y2].astype(BF16)
        S1[u, 0] = far[:, :128]
        S1[u, 1] = far[:, 128:]
        r1(u, 0).start()
        r1(u, 1).start()
        row = TG[k][0:1]
        sub, _ = iotas((256, 128))
        one_hot = (sub == row).astype(F32).astype(BF16)
        wanted = lax.dot_general(one_hot, TT[h], (((0,), (0,)), ((), ())), preferred_element_type=F32)
        PF[slot, y] = PF[slot, y] - wanted[:PIECE]

        @pl.when(u == 1)
        def _():
            xc[0].wait_recv()
            xc[5].start()
            xc[1].wait_recv()
            xc[6].start()

    def reduce_step(u):
        slot = lax.rem(u, 8)
        r1(u, 0).wait_recv()
        r1(u, 1).wait_recv()
        S2[u, 0, :, :128] = (PF[slot, yp, :, :128] + R1[u, 0].astype(F32)).astype(BF16)
        S2[u, 0, :, 128:] = PF[slot, yp, :, 128:].astype(BF16)
        r2(u, 0).start()
        S2[u, 1, :, :128] = PF[slot, ym, :, :128].astype(BF16)
        S2[u, 1, :, 128:] = (PF[slot, ym, :, 128:] + R1[u, 1].astype(F32)).astype(BF16)
        r2(u, 1).start()

    def error_step(u):
        k, h = unit(u)
        slot = lax.rem(u, 8)
        r2(u, 0).wait_recv()
        r2(u, 1).wait_recv()
        total = PF[slot, y] + R2[u, 0].astype(F32) + R2[u, 1].astype(F32)
        E[k, h, y] = (total * (1.0 / ROWS)).astype(BF16)
        a1(u, 0, y).start()
        a1(u, 1, y).start()

    def spread_step(u):
        a1(u, 0, ym).wait_recv()
        a2(u, 0, ym).start()
        a1(u, 1, yp).wait_recv()
        a2(u, 1, yp).start()

    def grad_step(u):
        k, h = unit(u)
        a2(u, 0, y2).wait_recv()
        a2(u, 1, y2).wait_recv()
        err = E[k, h].reshape(ROWS, HALF)
        G[k, h] = lax.dot_general(err, X[k], (((0,), (0,)), ((), ())), preferred_element_type=F32)
        for kk in range(8):

            @pl.when(k == kk)
            def _():
                def block(i, sums):
                    rows = pl.ds(pl.multiple_of(i * 8, 8), 8)
                    sums = list(sums)
                    for j in range(FEAT // 128):
                        cols = pl.ds(j * 128, 128)
                        mine = G[kk, h, rows, cols]
                        for l in range(kk):
                            sums[l] = sums[l] + mine * G[l, h, rows, cols]
                        sums[kk] = sums[kk] + mine * mine
                    return tuple(sums)

                sums = lax.fori_loop(
                    0, HALF // 8, block, tuple(jnp.zeros((8, 128), F32) for _ in range(kk + 1))
                )
                for l in range(kk + 1):
                    GA[kk, l] += sums[l]

        for d in range(2):
            r1(u, d).wait_send()
            r2(u, d).wait_send()
            a1(u, d, y).wait_send()
            a2(u, d, ym if d == 0 else yp).wait_send()

    def turn(t, carry):
        for n, step in ((3, spread_step), (2, error_step), (1, reduce_step), (0, forward), (4, grad_step)):

            @pl.when((t >= n * LAG) & (t < UNITS + n * LAG))
            def _():
                step(t - n * LAG)

        return carry

    lax.fori_loop(0, UNITS + 4 * LAG, turn, 0)

    def sum_xc(value, s):
        AX[s, 0] = value
        copies = []
        for k in range(1, 8):
            there = place_of(-KX[k], KC[k])
            cp = remote(AX.at[s, 0], AX.at[s, there], a_s.at[s, k], a_r.at[s, there], xcat(KX[k], KC[k]))
            cp.start()
            copies.append(cp)
        for cp in copies:
            cp.wait()
        return functools.reduce(jnp.add, [AX[s, k] for k in range(8)])

    def sum_y(value, s):
        AY[s, 0] = value
        copies = []
        for d in range(1, 4):
            cp = remote(AY.at[s, 0], AY.at[s, 4 - d], a_s.at[2 + s, d], a_r.at[2 + s, 4 - d], yat(d))
            cp.start()
            copies.append(cp)
        for cp in copies:
            cp.wait()
        return functools.reduce(jnp.add, [AY[s, k] for k in range(4)])

    def sum_z(value):
        AZ[0] = value
        copies = []
        for d in range(1, 8):
            cp = remote(AZ.at[0], AZ.at[8 - d], a_s.at[4, d], a_r.at[4, 8 - d], zat(d))
            cp.start()
            copies.append(cp)
        for cp in copies:
            cp.wait()
        return functools.reduce(jnp.add, [AZ[k] for k in range(8)])

    def replica(k):
        return lax.rem(x + (KX[k] % 4), 4) * 2 + lax.rem(c + KC[k], 2)

    coef = tree_coefficients(sum_y(sum_xc(gram_matrix(GA, replica), 0), 0))
    weights = [pick(coef, replica(k)) for k in range(8)]

    ccopies = {}
    for p in (7, 5, 6, 3, 4, 1, 2, 0):

        def mix(i, carry):
            rows = pl.ds(pl.multiple_of((p % 4) * 64 + i * 16, 16), 16)
            total = weights[0] * G[0, p // 4, rows, :]
            for k in range(1, 8):
                total = total + weights[k] * G[k, p // 4, rows, :]
            here = pl.ds(pl.multiple_of(i * 16, 16), 16)
            if p == 0:
                OWN[here, :] = total
            else:
                CS[p, here, :] = total.astype(BF16)
            return carry

        lax.fori_loop(0, 4, mix, 0)
        if p:
            there = block_of(-DZ[p])
            ccopies[there] = remote(CS.at[p], CB.at[there], c_s.at[p], c_r.at[there], zat(DZ[p]))
            ccopies[there].start()

    for p in range(8):
        if p:
            ccopies[p].wait_recv()

        def block(i, sums, p=p):
            rows = pl.ds(pl.multiple_of(i * 16, 16), 16)
            sums = list(sums)
            for j in range(FEAT // 128):
                cols = pl.ds(j * 128, 128)

                def read(q):
                    return CB[q, rows, cols].astype(F32) if q else OWN[rows, cols]

                mine = read(p)
                for l in range(p + 1):
                    prod = mine * read(l)
                    sums[l] = sums[l] + prod[:8] + prod[8:]
            return tuple(sums)

        sums = lax.fori_loop(0, 4, block, tuple(jnp.zeros((8, 128), F32) for _ in range(p + 1)))
        for l in range(p + 1):
            GB[p, l] = sums[l]

    def plane(p):
        return lax.rem(z + (DZ[p] % 8), 8)

    coef = tree_coefficients(sum_z(sum_y(sum_xc(gram_matrix(GB, plane), 1), 1)))
    weights = [pick(coef, plane(p)) for p in range(8)]

    def final(i, carry):
        rows = pl.ds(pl.multiple_of(i * 16, 16), 16)
        total = weights[0] * OWN[rows, :]
        for p in range(1, 8):
            total = total + weights[p] * CB[p, rows, :].astype(F32)
        out_ref[rows, :] = total
        return carry

    lax.fori_loop(0, 4, final, 0)

    for cp in wcopies + xc + list(ccopies.values()):
        cp.wait_send()


def on_device(inputs, weight, table, targets):
    vmem = pl.BlockSpec(memory_space=pltpu.VMEM)
    anywhere = pl.BlockSpec(memory_space=pl.ANY)
    dma = pltpu.SemaphoreType.DMA
    combined_t = pl.pallas_call(
        kernel,
        out_shape=jax.ShapeDtypeStruct((64, FEAT), F32),
        in_specs=[anywhere, vmem, vmem, anywhere],
        out_specs=vmem,
        scratch_shapes=[
            pltpu.VMEM((8, ROWS, FEAT), BF16),
            pltpu.VMEM((2, 4, 64, FEAT), BF16),
            pltpu.VMEM((8, 8, 128), jnp.int32),
            pltpu.VMEM((8, 256, 128), BF16),
            pltpu.VMEM((2, 256, HALF), BF16),
            pltpu.VMEM((8, 4, PIECE, HALF), F32),
            pltpu.VMEM((UNITS, 2, PIECE, 128), BF16),
            pltpu.VMEM((UNITS, 2, PIECE, HALF), BF16),
            pltpu.VMEM((UNITS, 2, PIECE, 128), BF16),
            pltpu.VMEM((UNITS, 2, PIECE, HALF), BF16),
            pltpu.VMEM((8, 2, 4, PIECE, HALF), BF16),
            pltpu.VMEM((8, 2, HALF, FEAT), F32),
            pltpu.VMEM((8, 8, 8, 128), F32),
            pltpu.VMEM((8, 8, 8, 128), F32),
            pltpu.VMEM((8, 64, FEAT), BF16),
            pltpu.VMEM((8, 64, FEAT), BF16),
            pltpu.VMEM((64, FEAT), F32),
            pltpu.VMEM((2, 8, 8, 128), F32),
            pltpu.VMEM((2, 4, 8, 128), F32),
            pltpu.VMEM((8, 8, 128), F32),
            dma((9,)),
            dma((8,)),
            dma((8,)),
            dma((10,)),
            dma((10,)),
            dma((7,)),
            dma((7,)),
            dma((4, 2, UNITS)),
            dma((4, 2, UNITS)),
            dma((8,)),
            dma((8,)),
            dma((5, 8)),
            dma((5, 8)),
        ],
        compiler_params=pltpu.CompilerParams(
            collective_id=0, has_side_effects=True, vmem_limit_bytes=56 * 1024 * 1024
        ),
    )(inputs, weight.T, targets[None], table)
    combined = combined_t.T
    return combined, weight - STEP * combined


def solution(mesh):
    split = Mesh(mesh.devices.reshape(8, 4, 2, mesh.shape["shard"]), AXES)
    return jax.shard_map(
        on_device,
        mesh=split,
        in_specs=(P(REP, "shard"), P("shard", REP), P(), P(REP + ("shard",))),
        out_specs=(P("shard", REP), P("shard", REP)),
        check_vma=False,
    )
```

```python
import functools

import jax
import jax.numpy as jnp
from jax import lax
from jax.experimental import pallas as pl
from jax.experimental.pallas import tpu as pltpu
from jax.sharding import Mesh
from jax.sharding import PartitionSpec as P

AXES = ("z", "x", "c", "shard")
REP = ("z", "x", "c")
MESH = pl.DeviceIdType.MESH
F32, BF16 = jnp.float32, jnp.bfloat16

EPS = 1e-06
STEP = 0.05

KX = (0, 0, -1, 1, -1, 1, 2, 2)
KC = (0, 1, 0, 0, 1, 1, 0, 1)
DZ = (0, -1, 1, -2, 2, -3, 3, 4)

ROWS, FEAT, PIECE, HALF = 320, 1024, 80, 256
UNITS, LAG = 16, 2


def place_of(steps, other):
    return [i for i in range(8) if KX[i] % 4 == steps % 4 and KC[i] == other][0]


def block_of(steps):
    return [i for i in range(8) if DZ[i] % 8 == steps % 8][0]


def iotas(shape):
    return lax.broadcasted_iota(jnp.int32, shape, 0), lax.broadcasted_iota(jnp.int32, shape, 1)


def swap_bit(v, bit, axis):
    pos = lax.broadcasted_iota(jnp.int32, v.shape, axis)
    up = pltpu.roll(v, bit, axis)
    down = pltpu.roll(v, v.shape[axis] - bit, axis)
    return jnp.where((pos & bit) != 0, up, down)


def tree_coefficients(gram):
    sub, lane = iotas(gram.shape)
    coef = jnp.ones((8, 1), F32)
    for bit in (1, 2, 4):
        own = jnp.where(lane == sub, gram, 0.0)
        cross = jnp.where(lane == (sub ^ bit), gram, 0.0)

        def factor(axis):
            norm = jnp.maximum(jnp.sum(own, axis=axis, keepdims=True), 0.0)
            return 1.0 - jnp.sum(cross, axis=axis, keepdims=True) / (2.0 * (norm + EPS))

        by_row, by_col = factor(1), factor(0)
        coef = coef * by_row
        gram = gram * by_row * by_col
        gram = gram + swap_bit(gram, bit, 1)
        gram = gram + swap_bit(gram, bit, 0)
    return coef


def pick(coef, index):
    sub, _ = iotas((8, 1))
    return jnp.sum(jnp.where(sub == index, coef, 0.0), axis=0, keepdims=True)


def gram_matrix(sums, index_of):
    sub, lane = iotas((8, 128))
    gram = jnp.zeros((8, 128), F32)
    for a in range(8):
        for b in range(a + 1):
            v = jnp.sum(jnp.sum(sums[a, b], axis=0, keepdims=True), axis=1, keepdims=True)
            i, j = index_of(a), index_of(b)
            here = ((sub == i) & (lane == j)) | ((sub == j) & (lane == i))
            gram = jnp.where(here, v, gram)
    return gram


def kernel(
    x_ref, w_ref, tgt_ref, table_ref, near_ref, far_ref,
    X, W, TG, TB, TT, PF, S1, S2, R1, R2, E, G, GA, GB, CS, CB, OWN, AC, AX, AZ,
    loc_sem, w_s, w_r, x_s, x_r, t_s, t_r, y_s, y_r, c_s, c_r, a_s, a_r,
):
    z, x = lax.axis_index("z"), lax.axis_index("x")
    c, y = lax.axis_index("c"), lax.axis_index("shard")

    def zat(d):
        return {"z": lax.rem(z + (d % 8), 8)}

    def yat(d):
        return {"shard": lax.rem(y + (d % 4), 4)}

    def xcat(d, o):
        dev = {}
        if d % 4:
            dev["x"] = lax.rem(x + (d % 4), 4)
        if o:
            dev["c"] = 1 - c
        return dev

    def xyat(d, e):
        return {"x": lax.rem(x + (d % 4), 4), "shard": lax.rem(y + (e % 4), 4)}

    def remote(src, dst, ssem, rsem, dev):
        return pltpu.make_async_remote_copy(
            src_ref=src, dst_ref=dst, send_sem=ssem, recv_sem=rsem, device_id=dev, device_id_type=MESH
        )

    barrier = pltpu.get_barrier_semaphore()
    others = [zat(d) for d in (4, 3, 5, 2, 6, 1, 7)]
    others += [xyat(d, e) for d in range(4) for e in range(4) if d or e]
    others += [xcat(d, 1) for d in range(4)]
    for dev in others:
        pl.semaphore_signal(barrier, inc=1, device_id=dev, device_id_type=MESH)
    TG[0] = jnp.zeros((8, 128), jnp.int32)
    TG[0, 0:1, 0:PIECE] = tgt_ref[...]

    own_x = pltpu.make_async_copy(x_ref, X.at[0], loc_sem.at[8])
    own_x.start()
    blocks = []
    for p in range(8):
        col = lax.rem(z + (DZ[p] % 8), 8) * 512 + x * 128
        cp = pltpu.make_async_copy(
            table_ref.at[:, pl.ds(pl.multiple_of(col, 128), 128)], TB.at[p], loc_sem.at[p]
        )
        cp.start()
        blocks.append(cp)

    W[0, 0] = w_ref[...].astype(BF16)
    GA[...] = jnp.zeros_like(GA)

    for cp in blocks:
        cp.wait()
    _, lane = iotas((256, 128))
    for q in range(4):
        left = pltpu.roll(TB[2 * q].astype(F32), 64 * c, 1)
        right = pltpu.roll(TB[2 * q + 1].astype(F32), 64 * (1 - c), 1)
        TT[q // 2, :, (q % 2) * 128 : (q % 2) * 128 + 128] = jnp.where(lane < 64, left, right).astype(BF16)

    own_x.wait()
    pl.semaphore_wait(barrier, len(others))

    def wslot(d):
        p = block_of(d)
        return W.at[p // 4, p % 4]

    def wcopy(i):
        n, sign = i // 2 + 1, (1 if i % 2 == 0 else -1)
        src = wslot(0) if n <= 2 else wslot(-sign * 2)
        dst = wslot(-sign * n)
        if n == 4:
            rows = pl.ds(0, 32) if sign == 1 else pl.ds(32, 32)
            src, dst = src.at[rows], dst.at[rows]
        return remote(src, dst, w_s.at[i], w_r.at[i], zat(sign * (n if n <= 2 else n - 2)))

    wcopies = [wcopy(i) for i in range(8)]
    for i in range(4):
        wcopies[i].start()

    lo, hi = pl.ds(0, 160), pl.ds(160, 160)
    xc = [
        remote(X.at[0, lo], X.at[2, lo], x_s.at[0], x_r.at[0], xcat(1, 0)),
        remote(X.at[0, hi], X.at[3, hi], x_s.at[1], x_r.at[1], xcat(-1, 0)),
        remote(X.at[0], X.at[1], x_s.at[2], x_r.at[2], xcat(0, 1)),
        remote(X.at[0, hi], X.at[2, hi], x_s.at[3], x_r.at[3], xcat(1, 0)),
        remote(X.at[0, lo], X.at[3, lo], x_s.at[4], x_r.at[4], xcat(-1, 0)),
        remote(X.at[2, lo], X.at[6, lo], x_s.at[5], x_r.at[5], xcat(1, 0)),
        remote(X.at[3, hi], X.at[6, hi], x_s.at[6], x_r.at[6], xcat(-1, 0)),
        remote(X.at[2], X.at[4], x_s.at[7], x_r.at[7], xcat(0, 1)),
        remote(X.at[3], X.at[5], x_s.at[8], x_r.at[8], xcat(0, 1)),
        remote(X.at[6], X.at[7], x_s.at[9], x_r.at[9], xcat(0, 1)),
    ]
    for i in range(5):
        xc[i].start()

    tcopies = []
    for k in range(1, 8):
        there = place_of(-KX[k], KC[k])
        tc = remote(TG.at[0], TG.at[there], t_s.at[k - 1], t_r.at[there - 1], xcat(KX[k], KC[k]))
        tc.start()
        tcopies.append(tc)
    for tc in tcopies:
        tc.wait()

    for i in (0, 1):
        wcopies[i].wait_recv()
    for i in (2, 3):
        wcopies[i].wait_recv()
        wcopies[i + 2].start()
        wcopies[i + 4].start()

    yp, ym, y2 = lax.rem(y + 1, 4), lax.rem(y + 3, 4), lax.rem(y + 2, 4)

    def unit(u):
        early = u < 4
        k = jnp.where(early, lax.rem(u, 2), u // 2)
        h = jnp.where(early, u // 2, lax.rem(u, 2))
        return k, h

    def r1(u, d):
        return remote(S1.at[u, d], R1.at[u, d], y_s.at[0, d, u], y_r.at[0, d, u], yat(1 - 2 * d))

    def r2(u, d):
        return remote(S2.at[u, d], R2.at[u, d], y_s.at[1, d, u], y_r.at[1, d, u], yat(1 - 2 * d))

    def a1(u, d, who):
        k, h = unit(u)
        ref = E.at[k, h, who]
        return remote(ref, ref, y_s.at[2, d, u], y_r.at[2, d, u], yat(1 - 2 * d))

    def a2(u, d, who):
        k, h = unit(u)
        ref = E.at[k, h, who, :, pl.ds(128 * d, 128)]
        return remote(ref, ref, y_s.at[3, d, u], y_r.at[3, d, u], yat(1 - 2 * d))

    def forward(u):
        k, h = unit(u)
        slot = lax.rem(u, 8)

        @pl.when(u == 1)
        def _():
            xc[2].wait_recv()

        @pl.when(u == 2)
        def _():
            for i in (4, 5, 6, 7):
                wcopies[i].wait_recv()

        @pl.when(u == 4)
        def _():
            xc[3].wait_recv()
            xc[7].start()

        @pl.when(u == 6)
        def _():
            xc[4].wait_recv()
            xc[8].start()

        @pl.when(u == 8)
        def _():
            xc[7].wait_recv()

        @pl.when(u == 10)
        def _():
            xc[8].wait_recv()

        @pl.when(u == 12)
        def _():
            xc[5].wait_recv()
            xc[6].wait_recv()
            xc[9].start()

        @pl.when(u == 14)
        def _():
            xc[9].wait_recv()

        part = lax.dot_general(
            X[k], W[h].reshape(HALF, FEAT), (((1,), (1,)), ((), ())), preferred_element_type=F32
        )
        PF[slot] = part.reshape(4, PIECE, HALF)
        far = PF[slot, y2].astype(BF16)
        S1[u, 0] = far[:, :128]
        S1[u, 1] = far[:, 128:]
        r1(u, 0).start()
        r1(u, 1).start()
        row = TG[k][0:1]
        sub, _ = iotas((256, 128))
        one_hot = (sub == row).astype(F32).astype(BF16)
        wanted = lax.dot_general(one_hot, TT[h], (((0,), (0,)), ((), ())), preferred_element_type=F32)
        PF[slot, y] = PF[slot, y] - wanted[:PIECE]

        @pl.when(u == 3)
        def _():
            xc[0].wait_recv()
            xc[5].start()
            xc[1].wait_recv()
            xc[6].start()

    def reduce_step(u):
        slot = lax.rem(u, 8)
        r1(u, 0).wait_recv()
        r1(u, 1).wait_recv()
        S2[u, 0, :, :128] = (PF[slot, yp, :, :128] + R1[u, 0].astype(F32)).astype(BF16)
        S2[u, 0, :, 128:] = PF[slot, yp, :, 128:].astype(BF16)
        r2(u, 0).start()
        S2[u, 1, :, :128] = PF[slot, ym, :, :128].astype(BF16)
        S2[u, 1, :, 128:] = (PF[slot, ym, :, 128:] + R1[u, 1].astype(F32)).astype(BF16)
        r2(u, 1).start()

    def error_step(u):
        k, h = unit(u)
        slot = lax.rem(u, 8)
        r2(u, 0).wait_recv()
        r2(u, 1).wait_recv()
        total = PF[slot, y] + R2[u, 0].astype(F32) + R2[u, 1].astype(F32)
        E[k, h, y] = (total * (1.0 / ROWS)).astype(BF16)
        a1(u, 0, y).start()
        a1(u, 1, y).start()

    def spread_step(u):
        a1(u, 0, ym).wait_recv()
        a2(u, 0, ym).start()
        a1(u, 1, yp).wait_recv()
        a2(u, 1, yp).start()

    def grad_step(u):
        k, h = unit(u)
        a2(u, 0, y2).wait_recv()
        a2(u, 1, y2).wait_recv()
        err = E[k, h].reshape(ROWS, HALF)
        G[k, h] = lax.dot_general(err, X[k], (((0,), (0,)), ((), ())), preferred_element_type=F32)
        for kk in range(8):

            @pl.when(k == kk)
            def _():
                def block(i, sums):
                    rows = pl.ds(pl.multiple_of(i * 8, 8), 8)
                    sums = list(sums)
                    for j in range(FEAT // 128):
                        cols = pl.ds(j * 128, 128)
                        mine = G[kk, h, rows, cols]
                        for l in range(kk):
                            sums[l] = sums[l] + mine * G[l, h, rows, cols]
                        sums[kk] = sums[kk] + mine * mine
                    return tuple(sums)

                sums = lax.fori_loop(
                    0, HALF // 8, block, tuple(jnp.zeros((8, 128), F32) for _ in range(kk + 1))
                )
                for l in range(kk + 1):
                    GA[kk, l] += sums[l]

        for d in range(2):
            r1(u, d).wait_send()
            r2(u, d).wait_send()
            a1(u, d, y).wait_send()
            a2(u, d, ym if d == 0 else yp).wait_send()

    def turn(t, carry):
        for n, step in ((3, spread_step), (2, error_step), (1, reduce_step), (0, forward), (4, grad_step)):

            @pl.when((t >= n * LAG) & (t < UNITS + n * LAG))
            def _():
                step(t - n * LAG)

        return carry

    lax.fori_loop(0, UNITS + 4 * LAG, turn, 0)

    def sum_plane(value, s):
        AC[s, 0] = value
        cp = remote(AC.at[s, 0], AC.at[s, 1], a_s.at[s, 0], a_r.at[s, 0], xcat(0, 1))
        cp.start()
        cp.wait()
        AX[s, 0] = AC[s, 0] + AC[s, 1]
        copies = []
        for i in range(1, 16):
            d, e = i // 4, i % 4
            there = (-d) % 4 * 4 + (-e) % 4
            cp = remote(AX.at[s, 0], AX.at[s, there], a_s.at[s, i], a_r.at[s, there], xyat(d, e))
            cp.start()
            copies.append(cp)
        for cp in copies:
            cp.wait()
        return jnp.sum(AX[s], axis=0)

    def sum_z(value):
        AZ[0] = value
        copies = []
        for d in range(1, 8):
            cp = remote(AZ.at[0], AZ.at[8 - d], a_s.at[2, d], a_r.at[2, 8 - d], zat(d))
            cp.start()
            copies.append(cp)
        for cp in copies:
            cp.wait()
        return functools.reduce(jnp.add, [AZ[k] for k in range(8)])

    def replica(k):
        return lax.rem(x + (KX[k] % 4), 4) * 2 + lax.rem(c + KC[k], 2)

    coef = tree_coefficients(sum_plane(gram_matrix(GA, replica), 0))
    weights = [pick(coef, replica(k)) for k in range(8)]

    ccopies = {}
    for p in (7, 5, 6, 3, 4, 1, 2, 0):

        def mix(i, carry):
            rows = pl.ds(pl.multiple_of((p % 4) * 64 + i * 16, 16), 16)
            total = weights[0] * G[0, p // 4, rows, :]
            for k in range(1, 8):
                total = total + weights[k] * G[k, p // 4, rows, :]
            here = pl.ds(pl.multiple_of(i * 16, 16), 16)
            if p == 0:
                OWN[here, :] = total
            else:
                CS[p, here, :] = total.astype(BF16)
            return carry

        lax.fori_loop(0, 4, mix, 0)
        if p:
            there = block_of(-DZ[p])
            ccopies[there] = remote(CS.at[p], CB.at[there], c_s.at[p], c_r.at[there], zat(DZ[p]))
            ccopies[there].start()

    for p in range(8):
        if p:
            ccopies[p].wait_recv()

        def block(i, sums, p=p):
            rows = pl.ds(pl.multiple_of(i * 16, 16), 16)
            sums = list(sums)
            for j in range(FEAT // 128):
                cols = pl.ds(j * 128, 128)

                def read(q):
                    return CB[q, rows, cols].astype(F32) if q else OWN[rows, cols]

                mine = read(p)
                for l in range(p + 1):
                    prod = mine * read(l)
                    sums[l] = sums[l] + prod[:8] + prod[8:]
            return tuple(sums)

        sums = lax.fori_loop(0, 4, block, tuple(jnp.zeros((8, 128), F32) for _ in range(p + 1)))
        for l in range(p + 1):
            GB[p, l] = sums[l]

    def plane(p):
        return lax.rem(z + (DZ[p] % 8), 8)

    coef = tree_coefficients(sum_z(sum_plane(gram_matrix(GB, plane), 1)))
    weights = [pick(coef, plane(p)) for p in range(8)]

    def final(i, carry):
        rows = pl.ds(pl.multiple_of(i * 16, 16), 16)
        near = weights[0] * OWN[rows, :]
        for p in range(1, 4):
            near = near + weights[p] * CB[p, rows, :].astype(F32)
        far = weights[4] * CB[4, rows, :].astype(F32)
        for p in range(5, 8):
            far = far + weights[p] * CB[p, rows, :].astype(F32)
        near_ref[rows, :] = near
        far_ref[rows, :] = far
        return carry

    lax.fori_loop(0, 4, final, 0)

    for cp in wcopies + xc + list(ccopies.values()):
        cp.wait_send()


def on_device(inputs, weight, table, targets):
    vmem = pl.BlockSpec(memory_space=pltpu.VMEM)
    anywhere = pl.BlockSpec(memory_space=pl.ANY)
    dma = pltpu.SemaphoreType.DMA
    near, far = pl.pallas_call(
        kernel,
        out_shape=[jax.ShapeDtypeStruct((64, FEAT), F32)] * 2,
        in_specs=[anywhere, vmem, vmem, anywhere],
        out_specs=[vmem] * 2,
        scratch_shapes=[
            pltpu.VMEM((8, ROWS, FEAT), BF16),
            pltpu.VMEM((2, 4, 64, FEAT), BF16),
            pltpu.VMEM((8, 8, 128), jnp.int32),
            pltpu.VMEM((8, 256, 128), BF16),
            pltpu.VMEM((2, 256, HALF), BF16),
            pltpu.VMEM((8, 4, PIECE, HALF), F32),
            pltpu.VMEM((UNITS, 2, PIECE, 128), BF16),
            pltpu.VMEM((UNITS, 2, PIECE, HALF), BF16),
            pltpu.VMEM((UNITS, 2, PIECE, 128), BF16),
            pltpu.VMEM((UNITS, 2, PIECE, HALF), BF16),
            pltpu.VMEM((8, 2, 4, PIECE, HALF), BF16),
            pltpu.VMEM((8, 2, HALF, FEAT), F32),
            pltpu.VMEM((8, 8, 8, 128), F32),
            pltpu.VMEM((8, 8, 8, 128), F32),
            pltpu.VMEM((8, 64, FEAT), BF16),
            pltpu.VMEM((8, 64, FEAT), BF16),
            pltpu.VMEM((64, FEAT), F32),
            pltpu.VMEM((2, 2, 8, 128), F32),
            pltpu.VMEM((2, 16, 8, 128), F32),
            pltpu.VMEM((8, 8, 128), F32),
            dma((9,)),
            dma((8,)),
            dma((8,)),
            dma((10,)),
            dma((10,)),
            dma((7,)),
            dma((7,)),
            dma((4, 2, UNITS)),
            dma((4, 2, UNITS)),
            dma((8,)),
            dma((8,)),
            dma((3, 16)),
            dma((3, 16)),
        ],
        compiler_params=pltpu.CompilerParams(
            collective_id=0, has_side_effects=True, vmem_limit_bytes=56 * 1024 * 1024
        ),
    )(inputs, weight.T, targets[None], table)
    combined = near + far
    return combined.T, (weight.T - STEP * combined).T


def solution(mesh):
    split = Mesh(mesh.devices.reshape(8, 4, 2, mesh.shape["shard"]), AXES)
    return jax.shard_map(
        on_device,
        mesh=split,
        in_specs=(P(REP, "shard"), P("shard", REP), P(), P(REP + ("shard",))),
        out_specs=(P("shard", REP), P("shard", REP)),
        check_vma=False,
    )
```

```python
import functools

import jax
import jax.numpy as jnp
from jax import lax
from jax.experimental import pallas as pl
from jax.experimental.pallas import tpu as pltpu
from jax.sharding import Mesh
from jax.sharding import PartitionSpec as P

AXES = ("z", "x", "c", "shard")
REP = ("z", "x", "c")
MESH = pl.DeviceIdType.MESH
F32, BF16 = jnp.float32, jnp.bfloat16

EPS = 1e-06
STEP = 0.05

KX = (0, 0, -1, 1, -1, 1, 2, 2)
KC = (0, 1, 0, 0, 1, 1, 0, 1)
DZ = (0, -1, 1, -2, 2, -3, 3, 4)

ROWS, FEAT, PIECE, HALF = 320, 1024, 80, 256
UNITS, LAG = 16, 2


def place_of(steps, other):
    return [i for i in range(8) if KX[i] % 4 == steps % 4 and KC[i] == other][0]


def block_of(steps):
    return [i for i in range(8) if DZ[i] % 8 == steps % 8][0]


def iotas(shape):
    return lax.broadcasted_iota(jnp.int32, shape, 0), lax.broadcasted_iota(jnp.int32, shape, 1)


def swap_bit(v, bit, axis):
    pos = lax.broadcasted_iota(jnp.int32, v.shape, axis)
    up = pltpu.roll(v, bit, axis)
    down = pltpu.roll(v, v.shape[axis] - bit, axis)
    return jnp.where((pos & bit) != 0, up, down)


def tree_coefficients(gram):
    sub, lane = iotas(gram.shape)
    coef = jnp.ones((8, 1), F32)
    for bit in (1, 2, 4):
        own = jnp.where(lane == sub, gram, 0.0)
        cross = jnp.where(lane == (sub ^ bit), gram, 0.0)

        def factor(axis):
            norm = jnp.maximum(jnp.sum(own, axis=axis, keepdims=True), 0.0)
            return 1.0 - jnp.sum(cross, axis=axis, keepdims=True) / (2.0 * (norm + EPS))

        by_row, by_col = factor(1), factor(0)
        coef = coef * by_row
        gram = gram * by_row * by_col
        gram = gram + swap_bit(gram, bit, 1)
        gram = gram + swap_bit(gram, bit, 0)
    return coef


def pick(coef, index):
    sub, _ = iotas((8, 1))
    return jnp.sum(jnp.where(sub == index, coef, 0.0), axis=0, keepdims=True)


def gram_matrix(sums, index_of):
    sub, lane = iotas((8, 128))
    gram = jnp.zeros((8, 128), F32)
    for a in range(8):
        for b in range(a + 1):
            v = jnp.sum(jnp.sum(sums[a, b], axis=0, keepdims=True), axis=1, keepdims=True)
            i, j = index_of(a), index_of(b)
            here = ((sub == i) & (lane == j)) | ((sub == j) & (lane == i))
            gram = jnp.where(here, v, gram)
    return gram


def kernel(
    x_ref, w_ref, tgt_ref, table_ref, near_ref, far_ref,
    X, W, TG, TB, TT, PF, S1, S2, R1, R2, E, G, GA, GB, CS, CB, OWN, AC, AX, AZ,
    loc_sem, w_s, w_r, x_s, x_r, t_s, t_r, y_s, y_r, c_s, c_r, a_s, a_r,
):
    z, x = lax.axis_index("z"), lax.axis_index("x")
    c, y = lax.axis_index("c"), lax.axis_index("shard")

    def zat(d):
        return {"z": lax.rem(z + (d % 8), 8)}

    def yat(d):
        return {"shard": lax.rem(y + (d % 4), 4)}

    def xcat(d, o):
        dev = {}
        if d % 4:
            dev["x"] = lax.rem(x + (d % 4), 4)
        if o:
            dev["c"] = 1 - c
        return dev

    def xyat(d, e):
        return {"x": lax.rem(x + (d % 4), 4), "shard": lax.rem(y + (e % 4), 4)}

    def remote(src, dst, ssem, rsem, dev):
        return pltpu.make_async_remote_copy(
            src_ref=src, dst_ref=dst, send_sem=ssem, recv_sem=rsem, device_id=dev, device_id_type=MESH
        )

    barrier = pltpu.get_barrier_semaphore()
    others = [zat(d) for d in (4, 3, 5, 2, 6, 1, 7)]
    others += [xyat(d, e) for d in range(4) for e in range(4) if d or e]
    others += [xcat(d, 1) for d in range(4)]
    for dev in others:
        pl.semaphore_signal(barrier, inc=1, device_id=dev, device_id_type=MESH)
    TG[0] = jnp.zeros((8, 128), jnp.int32)
    TG[0, 0:1, 0:PIECE] = tgt_ref[...]

    own_x = pltpu.make_async_copy(x_ref, X.at[0], loc_sem.at[8])
    own_x.start()
    blocks = []
    for p in range(8):
        col = lax.rem(z + (DZ[p] % 8), 8) * 512 + x * 128
        cp = pltpu.make_async_copy(
            table_ref.at[:, pl.ds(pl.multiple_of(col, 128), 128)], TB.at[p], loc_sem.at[p]
        )
        cp.start()
        blocks.append(cp)

    W[0, 0] = w_ref[...].astype(BF16)
    GA[...] = jnp.zeros_like(GA)

    for cp in blocks:
        cp.wait()
    _, lane = iotas((256, 128))
    for q in range(4):
        left = pltpu.roll(TB[2 * q].astype(F32), 64 * c, 1)
        right = pltpu.roll(TB[2 * q + 1].astype(F32), 64 * (1 - c), 1)
        TT[q // 2, :, (q % 2) * 128 : (q % 2) * 128 + 128] = jnp.where(lane < 64, left, right).astype(BF16)

    own_x.wait()
    pl.semaphore_wait(barrier, len(others))

    tcopies = []
    for k in range(1, 8):
        there = place_of(-KX[k], KC[k])
        tc = remote(TG.at[0], TG.at[there], t_s.at[k - 1], t_r.at[there - 1], xcat(KX[k], KC[k]))
        tc.start()
        tcopies.append(tc)
    def wslot(d):
        p = block_of(d)
        return W.at[p // 4, p % 4]

    def wcopy(i):
        n, sign = i // 2 + 1, (1 if i % 2 == 0 else -1)
        src = wslot(0) if n <= 2 else wslot(-sign * 2)
        dst = wslot(-sign * n)
        if n == 4:
            rows = pl.ds(0, 32) if sign == 1 else pl.ds(32, 32)
            src, dst = src.at[rows], dst.at[rows]
        return remote(src, dst, w_s.at[i], w_r.at[i], zat(sign * (n if n <= 2 else n - 2)))

    wcopies = [wcopy(i) for i in range(8)]
    for i in range(4):
        wcopies[i].start()

    lo, hi = pl.ds(0, 160), pl.ds(160, 160)
    xc = [
        remote(X.at[0, lo], X.at[2, lo], x_s.at[0], x_r.at[0], xcat(1, 0)),
        remote(X.at[0, hi], X.at[3, hi], x_s.at[1], x_r.at[1], xcat(-1, 0)),
        remote(X.at[0], X.at[1], x_s.at[2], x_r.at[2], xcat(0, 1)),
        remote(X.at[0, hi], X.at[2, hi], x_s.at[3], x_r.at[3], xcat(1, 0)),
        remote(X.at[0, lo], X.at[3, lo], x_s.at[4], x_r.at[4], xcat(-1, 0)),
        remote(X.at[2, lo], X.at[6, lo], x_s.at[5], x_r.at[5], xcat(1, 0)),
        remote(X.at[3, hi], X.at[6, hi], x_s.at[6], x_r.at[6], xcat(-1, 0)),
        remote(X.at[2], X.at[4], x_s.at[7], x_r.at[7], xcat(0, 1)),
        remote(X.at[3], X.at[5], x_s.at[8], x_r.at[8], xcat(0, 1)),
        remote(X.at[6], X.at[7], x_s.at[9], x_r.at[9], xcat(0, 1)),
    ]
    for i in range(5):
        xc[i].start()

    for i in (0, 1):
        wcopies[i].wait_recv()
    for i in (2, 3):
        wcopies[i].wait_recv()
        wcopies[i + 2].start()
        wcopies[i + 4].start()

    yp, ym, y2 = lax.rem(y + 1, 4), lax.rem(y + 3, 4), lax.rem(y + 2, 4)

    def unit(u):
        early = u < 4
        k = jnp.where(early, lax.rem(u, 2), u // 2)
        h = jnp.where(early, u // 2, lax.rem(u, 2))
        return k, h

    def r1(u, d):
        return remote(S1.at[u, d], R1.at[u, d], y_s.at[0, d, u], y_r.at[0, d, u], yat(1 - 2 * d))

    def r2(u, d):
        return remote(S2.at[u, d], R2.at[u, d], y_s.at[1, d, u], y_r.at[1, d, u], yat(1 - 2 * d))

    def a1(u, d, who):
        k, h = unit(u)
        ref = E.at[k, h, who]
        return remote(ref, ref, y_s.at[2, d, u], y_r.at[2, d, u], yat(1 - 2 * d))

    def a2(u, d, who):
        k, h = unit(u)
        ref = E.at[k, h, who, :, pl.ds(128 * d, 128)]
        return remote(ref, ref, y_s.at[3, d, u], y_r.at[3, d, u], yat(1 - 2 * d))

    def forward(u):
        k, h = unit(u)
        slot = lax.rem(u, 8)

        @pl.when(u == 1)
        def _():
            xc[2].wait_recv()

        @pl.when(u == 2)
        def _():
            for i in (4, 5, 6, 7):
                wcopies[i].wait_recv()

        @pl.when(u == 4)
        def _():
            xc[3].wait_recv()
            xc[7].start()

        @pl.when(u == 6)
        def _():
            xc[4].wait_recv()
            xc[8].start()

        @pl.when(u == 8)
        def _():
            xc[7].wait_recv()

        @pl.when(u == 10)
        def _():
            xc[8].wait_recv()

        @pl.when(u == 12)
        def _():
            xc[5].wait_recv()
            xc[6].wait_recv()
            xc[9].start()

        @pl.when(u == 14)
        def _():
            xc[9].wait_recv()

        part = lax.dot_general(
            X[k], W[h].reshape(HALF, FEAT), (((1,), (1,)), ((), ())), preferred_element_type=F32
        )
        PF[slot] = part.reshape(4, PIECE, HALF)
        far = PF[slot, y2].astype(BF16)
        S1[u, 0] = far[:, :128]
        S1[u, 1] = far[:, 128:]
        r1(u, 0).start()
        r1(u, 1).start()

        @pl.when(u == 0)
        def _():
            for tc in tcopies:
                tc.wait()

        row = TG[k][0:1]
        sub, _ = iotas((256, 128))
        one_hot = (sub == row).astype(F32).astype(BF16)
        wanted = lax.dot_general(one_hot, TT[h], (((0,), (0,)), ((), ())), preferred_element_type=F32)
        PF[slot, y] = PF[slot, y] - wanted[:PIECE]

        @pl.when(u == 3)
        def _():
            xc[0].wait_recv()
            xc[5].start()
            xc[1].wait_recv()
            xc[6].start()

    def reduce_step(u):
        slot = lax.rem(u, 8)
        r1(u, 0).wait_recv()
        r1(u, 1).wait_recv()
        S2[u, 0, :, :128] = (PF[slot, yp, :, :128] + R1[u, 0].astype(F32)).astype(BF16)
        S2[u, 0, :, 128:] = PF[slot, yp, :, 128:].astype(BF16)
        r2(u, 0).start()
        S2[u, 1, :, :128] = PF[slot, ym, :, :128].astype(BF16)
        S2[u, 1, :, 128:] = (PF[slot, ym, :, 128:] + R1[u, 1].astype(F32)).astype(BF16)
        r2(u, 1).start()

    def error_step(u):
        k, h = unit(u)
        slot = lax.rem(u, 8)
        r2(u, 0).wait_recv()
        r2(u, 1).wait_recv()
        total = PF[slot, y] + R2[u, 0].astype(F32) + R2[u, 1].astype(F32)
        E[k, h, y] = (total * (1.0 / ROWS)).astype(BF16)
        a1(u, 0, y).start()
        a1(u, 1, y).start()

    def spread_step(u):
        a1(u, 0, ym).wait_recv()
        a2(u, 0, ym).start()
        a1(u, 1, yp).wait_recv()
        a2(u, 1, yp).start()

    def grad_step(u):
        k, h = unit(u)
        a2(u, 0, y2).wait_recv()
        a2(u, 1, y2).wait_recv()
        err = E[k, h].reshape(ROWS, HALF)
        G[k, h] = lax.dot_general(err, X[k], (((0,), (0,)), ((), ())), preferred_element_type=F32)
        for kk in range(8):

            @pl.when(k == kk)
            def _():
                def block(i, sums):
                    rows = pl.ds(pl.multiple_of(i * 8, 8), 8)
                    sums = list(sums)
                    for j in range(FEAT // 128):
                        cols = pl.ds(j * 128, 128)
                        mine = G[kk, h, rows, cols]
                        for l in range(kk):
                            sums[l] = sums[l] + mine * G[l, h, rows, cols]
                        sums[kk] = sums[kk] + mine * mine
                    return tuple(sums)

                sums = lax.fori_loop(
                    0, HALF // 8, block, tuple(jnp.zeros((8, 128), F32) for _ in range(kk + 1))
                )
                for l in range(kk + 1):
                    GA[kk, l] += sums[l]

        for d in range(2):
            r1(u, d).wait_send()
            r2(u, d).wait_send()
            a1(u, d, y).wait_send()
            a2(u, d, ym if d == 0 else yp).wait_send()

    def turn(t, carry):
        for n, step in ((3, spread_step), (2, error_step), (1, reduce_step), (0, forward), (4, grad_step)):

            @pl.when((t >= n * LAG) & (t < UNITS + n * LAG))
            def _():
                step(t - n * LAG)

        return carry

    lax.fori_loop(0, UNITS + 4 * LAG, turn, 0)

    def sum_plane(value, s):
        AC[s, 0] = value
        cp = remote(AC.at[s, 0], AC.at[s, 1], a_s.at[s, 0], a_r.at[s, 0], xcat(0, 1))
        cp.start()
        cp.wait()
        AX[s, 0] = AC[s, 0] + AC[s, 1]
        copies = []
        for i in range(1, 16):
            d, e = i // 4, i % 4
            there = (-d) % 4 * 4 + (-e) % 4
            cp = remote(AX.at[s, 0], AX.at[s, there], a_s.at[s, i], a_r.at[s, there], xyat(d, e))
            cp.start()
            copies.append(cp)
        for cp in copies:
            cp.wait()
        return jnp.sum(AX[s], axis=0)

    def sum_z(value):
        AZ[0] = value
        copies = []
        for d in range(1, 8):
            cp = remote(AZ.at[0], AZ.at[8 - d], a_s.at[2, d], a_r.at[2, 8 - d], zat(d))
            cp.start()
            copies.append(cp)
        for cp in copies:
            cp.wait()
        return functools.reduce(jnp.add, [AZ[k] for k in range(8)])

    def replica(k):
        return lax.rem(x + (KX[k] % 4), 4) * 2 + lax.rem(c + KC[k], 2)

    coef = tree_coefficients(sum_plane(gram_matrix(GA, replica), 0))
    weights = [pick(coef, replica(k)) for k in range(8)]

    ccopies = {}
    for p in (7, 5, 6, 3, 4, 1, 2, 0):

        def mix(i, carry):
            rows = pl.ds(pl.multiple_of((p % 4) * 64 + i * 16, 16), 16)
            total = weights[0] * G[0, p // 4, rows, :]
            for k in range(1, 8):
                total = total + weights[k] * G[k, p // 4, rows, :]
            here = pl.ds(pl.multiple_of(i * 16, 16), 16)
            if p == 0:
                OWN[here, :] = total
            else:
                CS[p, here, :] = total.astype(BF16)
            return carry

        lax.fori_loop(0, 4, mix, 0)
        if p:
            there = block_of(-DZ[p])
            ccopies[there] = remote(CS.at[p], CB.at[there], c_s.at[p], c_r.at[there], zat(DZ[p]))
            ccopies[there].start()

    for p in range(8):
        if p:
            ccopies[p].wait_recv()

        def block(i, sums, p=p):
            rows = pl.ds(pl.multiple_of(i * 16, 16), 16)
            sums = list(sums)
            for j in range(FEAT // 128):
                cols = pl.ds(j * 128, 128)

                def read(q):
                    return CB[q, rows, cols].astype(F32) if q else OWN[rows, cols]

                mine = read(p)
                for l in range(p + 1):
                    prod = mine * read(l)
                    sums[l] = sums[l] + prod[:8] + prod[8:]
            return tuple(sums)

        sums = lax.fori_loop(0, 4, block, tuple(jnp.zeros((8, 128), F32) for _ in range(p + 1)))
        for l in range(p + 1):
            GB[p, l] = sums[l]

    def plane(p):
        return lax.rem(z + (DZ[p] % 8), 8)

    coef = tree_coefficients(sum_z(sum_plane(gram_matrix(GB, plane), 1)))
    weights = [pick(coef, plane(p)) for p in range(8)]

    def final(i, carry):
        rows = pl.ds(pl.multiple_of(i * 16, 16), 16)
        near = weights[0] * OWN[rows, :]
        for p in range(1, 4):
            near = near + weights[p] * CB[p, rows, :].astype(F32)
        far = weights[4] * CB[4, rows, :].astype(F32)
        for p in range(5, 8):
            far = far + weights[p] * CB[p, rows, :].astype(F32)
        near_ref[rows, :] = near
        far_ref[rows, :] = far
        return carry

    lax.fori_loop(0, 4, final, 0)

    for cp in wcopies + xc + list(ccopies.values()):
        cp.wait_send()


def on_device(inputs, weight, table, targets):
    vmem = pl.BlockSpec(memory_space=pltpu.VMEM)
    anywhere = pl.BlockSpec(memory_space=pl.ANY)
    dma = pltpu.SemaphoreType.DMA
    near, far = pl.pallas_call(
        kernel,
        out_shape=[jax.ShapeDtypeStruct((64, FEAT), F32)] * 2,
        in_specs=[anywhere, vmem, vmem, anywhere],
        out_specs=[vmem] * 2,
        scratch_shapes=[
            pltpu.VMEM((8, ROWS, FEAT), BF16),
            pltpu.VMEM((2, 4, 64, FEAT), BF16),
            pltpu.VMEM((8, 8, 128), jnp.int32),
            pltpu.VMEM((8, 256, 128), BF16),
            pltpu.VMEM((2, 256, HALF), BF16),
            pltpu.VMEM((8, 4, PIECE, HALF), F32),
            pltpu.VMEM((UNITS, 2, PIECE, 128), BF16),
            pltpu.VMEM((UNITS, 2, PIECE, HALF), BF16),
            pltpu.VMEM((UNITS, 2, PIECE, 128), BF16),
            pltpu.VMEM((UNITS, 2, PIECE, HALF), BF16),
            pltpu.VMEM((8, 2, 4, PIECE, HALF), BF16),
            pltpu.VMEM((8, 2, HALF, FEAT), F32),
            pltpu.VMEM((8, 8, 8, 128), F32),
            pltpu.VMEM((8, 8, 8, 128), F32),
            pltpu.VMEM((8, 64, FEAT), BF16),
            pltpu.VMEM((8, 64, FEAT), BF16),
            pltpu.VMEM((64, FEAT), F32),
            pltpu.VMEM((2, 2, 8, 128), F32),
            pltpu.VMEM((2, 16, 8, 128), F32),
            pltpu.VMEM((8, 8, 128), F32),
            dma((9,)),
            dma((8,)),
            dma((8,)),
            dma((10,)),
            dma((10,)),
            dma((7,)),
            dma((7,)),
            dma((4, 2, UNITS)),
            dma((4, 2, UNITS)),
            dma((8,)),
            dma((8,)),
            dma((3, 16)),
            dma((3, 16)),
        ],
        compiler_params=pltpu.CompilerParams(
            collective_id=0, has_side_effects=True, vmem_limit_bytes=56 * 1024 * 1024
        ),
    )(inputs, weight.T, targets[None], table)
    combined = near + far
    return combined.T, (weight.T - STEP * combined).T


def solution(mesh):
    split = Mesh(mesh.devices.reshape(8, 4, 2, mesh.shape["shard"]), AXES)
    return jax.shard_map(
        on_device,
        mesh=split,
        in_specs=(P(REP, "shard"), P("shard", REP), P(), P(REP + ("shard",))),
        out_specs=(P("shard", REP), P("shard", REP)),
        check_vma=False,
    )
```

```python
import functools

import jax
import jax.numpy as jnp
from jax import lax
from jax.experimental import pallas as pl
from jax.experimental.pallas import tpu as pltpu
from jax.sharding import Mesh
from jax.sharding import PartitionSpec as P

AXES = ("z", "x", "c", "shard")
REP = ("z", "x", "c")
MESH = pl.DeviceIdType.MESH
F32, BF16 = jnp.float32, jnp.bfloat16

EPS = 1e-06
STEP = 0.05

KX = (0, 0, -1, 1, -1, 1, 0, 0, 2, 2, -1, 1, -1, 1, 2, 2)
KC = (0, 1, 0, 0, 1, 1, 0, 1, 0, 1, 0, 0, 1, 1, 0, 1)
KM = (0, 0, 0, 0, 0, 0, 1, 1, 0, 0, 1, 1, 1, 1, 1, 1)
DZ = (0, 2, -2, 4)

ROWS, FEAT, PIECE, HALF = 320, 1024, 80, 256
UNITS, LAG = 16, 2


def place_of(steps, other, plane):
    return [i for i in range(16) if (KX[i] % 4, KC[i], KM[i]) == (steps % 4, other, plane)][0]


def block_of(steps):
    return [i for i in range(4) if DZ[i] % 8 == steps % 8][0]


def iotas(shape):
    return lax.broadcasted_iota(jnp.int32, shape, 0), lax.broadcasted_iota(jnp.int32, shape, 1)


def swap_bit(v, bit, axis):
    pos = lax.broadcasted_iota(jnp.int32, v.shape, axis)
    up = pltpu.roll(v, bit, axis)
    down = pltpu.roll(v, v.shape[axis] - bit, axis)
    return jnp.where((pos & bit) != 0, up, down)


def tree_coefficients(gram, bits):
    sub, lane = iotas(gram.shape)
    coef = jnp.ones((gram.shape[0], 1), F32)
    for bit in bits:
        own = jnp.where(lane == sub, gram, 0.0)
        cross = jnp.where(lane == (sub ^ bit), gram, 0.0)

        def factor(axis):
            norm = jnp.maximum(jnp.sum(own, axis=axis, keepdims=True), 0.0)
            return 1.0 - jnp.sum(cross, axis=axis, keepdims=True) / (2.0 * (norm + EPS))

        by_row, by_col = factor(1), factor(0)
        coef = coef * by_row
        gram = gram * by_row * by_col
        gram = gram + swap_bit(gram, bit, 1)
        gram = gram + swap_bit(gram, bit, 0)
    return coef


def pick(coef, index):
    sub, _ = iotas(coef.shape)
    return jnp.sum(jnp.where(sub == index, coef, 0.0), axis=0, keepdims=True)


def put_pair(gram, i, j, products):
    sub, lane = iotas(gram.shape)
    v = jnp.sum(jnp.sum(products, axis=0, keepdims=True), axis=1, keepdims=True)
    return jnp.where(((sub == i) & (lane == j)) | ((sub == j) & (lane == i)), v, gram)


def kernel(
    x_ref, w_ref, tgt_ref, table_ref, near_ref, far_ref,
    X, W, TG, TB, TT, PF, S1, S2, R1, R2, E, G, GA, CS, CB, OWN, AC, AX, BC, BX, AZ,
    loc_sem, w_s, w_r, z_s, z_r, x_s, x_r, t_s, t_r, y_s, y_r, c_s, c_r, a_s, a_r,
):
    z, x = lax.axis_index("z"), lax.axis_index("x")
    c, y = lax.axis_index("c"), lax.axis_index("shard")

    def zat(d):
        return {"z": lax.rem(z + (d % 8), 8)}

    def yat(d):
        return {"shard": lax.rem(y + (d % 4), 4)}

    def xcat(d, o):
        dev = {}
        if d % 4:
            dev["x"] = lax.rem(x + (d % 4), 4)
        if o:
            dev["c"] = 1 - c
        return dev

    mine = lax.rem(z, 2)

    def partner(o):
        dev = {"z": z + 1 - 2 * mine}
        if o:
            dev["c"] = 1 - c
        return dev

    def xyat(d, e):
        return {"x": lax.rem(x + (d % 4), 4), "shard": lax.rem(y + (e % 4), 4)}

    def remote(src, dst, ssem, rsem, dev):
        return pltpu.make_async_remote_copy(
            src_ref=src, dst_ref=dst, send_sem=ssem, recv_sem=rsem, device_id=dev, device_id_type=MESH
        )

    barrier = pltpu.get_barrier_semaphore()
    others = [zat(d) for d in (4, 3, 5, 2, 6, 1, 7)]
    others += [xyat(d, e) for d in range(4) for e in range(4) if d or e]
    others += [xcat(d, 1) for d in range(4)] + [partner(1)]
    for dev in others:
        pl.semaphore_signal(barrier, inc=1, device_id=dev, device_id_type=MESH)
    TG[0] = jnp.zeros((8, 128), jnp.int32)
    TG[0, 0:1, 0:PIECE] = tgt_ref[...]

    own_x = pltpu.make_async_copy(x_ref, X.at[0], loc_sem.at[4])
    own_x.start()
    blocks = []
    for p in range(4):
        col = lax.rem(z + (DZ[p] % 8), 8) * 512 + x * 128
        cp = pltpu.make_async_copy(
            table_ref.at[:, pl.ds(pl.multiple_of(col, 128), 128)], TB.at[p], loc_sem.at[p]
        )
        cp.start()
        blocks.append(cp)

    W[0] = w_ref[...].astype(BF16)
    GA[...] = jnp.zeros_like(GA)

    for cp in blocks:
        cp.wait()
    _, lane = iotas((256, 128))
    for q in range(2):
        left = pltpu.roll(TB[2 * q].astype(F32), 64 * c, 1)
        right = pltpu.roll(TB[2 * q + 1].astype(F32), 64 * (1 - c), 1)
        TT[:, q * 128 : q * 128 + 128] = jnp.where(lane < 64, left, right).astype(BF16)

    own_x.wait()
    pl.semaphore_wait(barrier, len(others))

    def target_copy(k, m):
        there = place_of(-KX[k], KC[k], m)
        slot = place_of(0, 0, m)
        return remote(TG.at[slot], TG.at[there], t_s.at[m, k], t_r.at[there], xcat(KX[k], KC[k]))

    others_in_plane = [k for k in range(1, 16) if KM[k] == 0]
    tpair = remote(TG.at[0], TG.at[6], t_s.at[0, 0], t_r.at[6], partner(0))
    tcopies = [[target_copy(k, m) for k in others_in_plane] for m in range(2)]
    tpair.start()
    for tc in tcopies[0]:
        tc.start()

    wcopies = []
    for p in range(1, 4):
        there = block_of(-DZ[p])
        wcopies.append(remote(W.at[0], W.at[there], w_s.at[p], w_r.at[there], zat(DZ[p])))
        wcopies[-1].start()

    lo, hi = pl.ds(0, 160), pl.ds(160, 160)
    xpair = [remote(X.at[0, h], X.at[6, h], z_s.at[i], z_r.at[i], partner(0)) for i, h in enumerate((lo, hi))]

    def around(m):
        own, core, left, right, far = (place_of(d, o, m) for d, o in ((0, 0), (0, 1), (-1, 0), (1, 0), (2, 0)))
        left_core, right_core, far_core = (place_of(d, 1, m) for d in (-1, 1, 2))
        plan = (
            (X.at[own, lo], X.at[left, lo], xcat(1, 0)),
            (X.at[own, hi], X.at[right, hi], xcat(-1, 0)),
            (X.at[own], X.at[core], xcat(0, 1)),
            (X.at[own, hi], X.at[left, hi], xcat(1, 0)),
            (X.at[own, lo], X.at[right, lo], xcat(-1, 0)),
            (X.at[left, lo], X.at[far, lo], xcat(1, 0)),
            (X.at[right, hi], X.at[far, hi], xcat(-1, 0)),
            (X.at[left], X.at[left_core], xcat(0, 1)),
            (X.at[right], X.at[right_core], xcat(0, 1)),
            (X.at[far], X.at[far_core], xcat(0, 1)),
        )
        return [remote(a, b, x_s.at[m, i], x_r.at[m, i], dev) for i, (a, b, dev) in enumerate(plan)]

    xa, xb = around(0), around(1)
    for i in range(5):
        xa[i].start()
    for cp in xpair:
        cp.start()

    tpair.wait_recv()
    for tc in tcopies[1]:
        tc.start()
    for cp in wcopies:
        cp.wait_recv()

    yp, ym, y2 = lax.rem(y + 1, 4), lax.rem(y + 3, 4), lax.rem(y + 2, 4)

    def r1(u, d):
        return remote(S1.at[u, d], R1.at[u, d], y_s.at[0, d, u], y_r.at[0, d, u], yat(1 - 2 * d))

    def r2(u, d):
        return remote(S2.at[u, d], R2.at[u, d], y_s.at[1, d, u], y_r.at[1, d, u], yat(1 - 2 * d))

    def a1(u, d, who):
        ref = E.at[u, who]
        return remote(ref, ref, y_s.at[2, d, u], y_r.at[2, d, u], yat(1 - 2 * d))

    def a2(u, d, who):
        ref = E.at[u, who, :, pl.ds(128 * d, 128)]
        return remote(ref, ref, y_s.at[3, d, u], y_r.at[3, d, u], yat(1 - 2 * d))

    def arrived(u):
        plan = {
            1: ((xa[2], None), (xa[0], xa[5]), (xa[1], xa[6])),
            2: ((xa[3], xa[7]),),
            3: ((xa[4], xa[8]),),
            4: ((xa[7], None), (xpair[0], xb[0], xb[4])),
            5: ((xa[8], None),),
            6: ((xpair[1], xb[1], xb[3], xb[2]),),
            7: ((xb[2], None),),
            8: ((xa[5], None), (xa[6], xa[9])),
            9: ((xa[9], None), (xb[0], xb[5])),
            10: ((xb[3], xb[7]), (xb[1], xb[6])),
            11: ((xb[4], xb[8]),),
            12: ((xb[7], None),),
            13: ((xb[8], None),),
            14: ((xb[5], None), (xb[6], xb[9])),
            15: ((xb[9], None),),
        }
        for turn, steps in plan.items():

            @pl.when(u == turn)
            def _(steps=steps):
                for first, *then in steps:
                    first.wait_recv()
                    for cp in then:
                        if cp is not None:
                            cp.start()

    def forward(u):
        slot = lax.rem(u, 8)
        arrived(u)
        part = lax.dot_general(
            X[u], W[...].reshape(HALF, FEAT), (((1,), (1,)), ((), ())), preferred_element_type=F32
        )
        PF[slot] = part.reshape(4, PIECE, HALF)
        far = PF[slot, y2].astype(BF16)
        S1[u, 0] = far[:, :128]
        S1[u, 1] = far[:, 128:]
        r1(u, 0).start()
        r1(u, 1).start()

        @pl.when(u == 0)
        def _():
            for tc in tcopies[0]:
                tc.wait_recv()

        @pl.when(u == 6)
        def _():
            for tc in tcopies[1]:
                tc.wait_recv()

        row = TG[u][0:1]
        sub, _ = iotas((256, 128))
        one_hot = (sub == row).astype(F32).astype(BF16)
        wanted = lax.dot_general(one_hot, TT[...], (((0,), (0,)), ((), ())), preferred_element_type=F32)
        PF[slot, y] = PF[slot, y] - wanted[:PIECE]

    def reduce_step(u):
        slot = lax.rem(u, 8)
        r1(u, 0).wait_recv()
        r1(u, 1).wait_recv()
        S2[u, 0, :, :128] = (PF[slot, yp, :, :128] + R1[u, 0].astype(F32)).astype(BF16)
        S2[u, 0, :, 128:] = PF[slot, yp, :, 128:].astype(BF16)
        r2(u, 0).start()
        S2[u, 1, :, :128] = PF[slot, ym, :, :128].astype(BF16)
        S2[u, 1, :, 128:] = (PF[slot, ym, :, 128:] + R1[u, 1].astype(F32)).astype(BF16)
        r2(u, 1).start()

    def error_step(u):
        slot = lax.rem(u, 8)
        r2(u, 0).wait_recv()
        r2(u, 1).wait_recv()
        total = PF[slot, y] + R2[u, 0].astype(F32) + R2[u, 1].astype(F32)
        E[u, y] = (total * (1.0 / ROWS)).astype(BF16)
        a1(u, 0, y).start()
        a1(u, 1, y).start()

    def spread_step(u):
        a1(u, 0, ym).wait_recv()
        a2(u, 0, ym).start()
        a1(u, 1, yp).wait_recv()
        a2(u, 1, yp).start()

    def replica(k):
        plane = lax.rem(mine + KM[k], 2)
        return plane * 8 + lax.rem(x + (KX[k] % 4), 4) * 2 + lax.rem(c + KC[k], 2)

    def grad_step(u):
        a2(u, 0, y2).wait_recv()
        a2(u, 1, y2).wait_recv()
        err = E[u].reshape(ROWS, HALF)
        G[u] = lax.dot_general(err, X[u], (((0,), (0,)), ((), ())), preferred_element_type=F32)
        for kk in range(16):

            @pl.when(u == kk)
            def _():
                def block(i, sums):
                    rows = pl.ds(pl.multiple_of(i * 8, 8), 8)
                    sums = list(sums)
                    for j in range(FEAT // 128):
                        cols = pl.ds(j * 128, 128)
                        own = G[kk, rows, cols]
                        for l in range(kk):
                            sums[l] = sums[l] + own * G[l, rows, cols]
                        sums[kk] = sums[kk] + own * own
                    return tuple(sums)

                sums = lax.fori_loop(
                    0, HALF // 8, block, tuple(jnp.zeros((8, 128), F32) for _ in range(kk + 1))
                )
                gram = GA[...]
                for l in range(kk + 1):
                    gram = put_pair(gram, replica(kk), replica(l), sums[l])
                GA[...] = gram

        for d in range(2):
            r1(u, d).wait_send()
            r2(u, d).wait_send()
            a1(u, d, y).wait_send()
            a2(u, d, ym if d == 0 else yp).wait_send()

    def turn(t, carry):
        for n, step in ((3, spread_step), (2, error_step), (1, reduce_step), (0, forward), (4, grad_step)):

            @pl.when((t >= n * LAG) & (t < UNITS + n * LAG))
            def _():
                step(t - n * LAG)

        return carry

    lax.fori_loop(0, UNITS + 4 * LAG, turn, 0)

    def sum_xy(ref, s):
        copies = []
        for i in range(1, 16):
            d, e = i // 4, i % 4
            there = (-d) % 4 * 4 + (-e) % 4
            cp = remote(ref.at[0], ref.at[there], a_s.at[s, i], a_r.at[s, there], xyat(d, e))
            cp.start()
            copies.append(cp)
        for cp in copies:
            cp.wait()
        return jnp.sum(ref[...], axis=0)

    def sum_planes(value):
        AC[0] = value
        near = (xcat(0, 1), partner(0), partner(1))
        copies = [remote(AC.at[0], AC.at[i + 1], a_s.at[3, i], a_r.at[3, i], dev) for i, dev in enumerate(near)]
        for cp in copies:
            cp.start()
        for cp in copies:
            cp.wait()
        AX[0] = jnp.sum(AC[...], axis=0)
        return sum_xy(AX, 0)

    def sum_plane(value):
        BC[0] = value
        cp = remote(BC.at[0], BC.at[1], a_s.at[4, 0], a_r.at[4, 0], xcat(0, 1))
        cp.start()
        cp.wait()
        BX[0] = BC[0] + BC[1]
        return sum_xy(BX, 1)

    def sum_z(value):
        AZ[0] = value
        copies = []
        for d in range(1, 8):
            cp = remote(AZ.at[0], AZ.at[8 - d], a_s.at[2, d], a_r.at[2, 8 - d], zat(d))
            cp.start()
            copies.append(cp)
        for cp in copies:
            cp.wait()
        return functools.reduce(jnp.add, [AZ[k] for k in range(8)])

    coef = tree_coefficients(sum_planes(GA[...]), (1, 2, 4, 8))
    weights = [pick(coef, replica(k)) for k in range(16)]

    ccopies = {}
    for p in (3, 1, 2, 0):

        def mix(i, carry):
            rows = pl.ds(pl.multiple_of(p * 64 + i * 16, 16), 16)
            total = weights[0] * G[0, rows, :]
            for k in range(1, 16):
                total = total + weights[k] * G[k, rows, :]
            here = pl.ds(pl.multiple_of(i * 16, 16), 16)
            if p == 0:
                OWN[here, :] = total
            else:
                CS[p, here, :] = total.astype(BF16)
            return carry

        lax.fori_loop(0, 4, mix, 0)
        if p:
            there = block_of(-DZ[p])
            ccopies[there] = remote(CS.at[p], CB.at[there], c_s.at[p], c_r.at[there], zat(DZ[p]))
            ccopies[there].start()

    def pair(p):
        return lax.rem(z + (DZ[p] % 8), 8) // 2

    gram = jnp.zeros((8, 128), F32)
    for p in range(4):
        if p:
            ccopies[p].wait_recv()

        def block(i, sums, p=p):
            rows = pl.ds(pl.multiple_of(i * 16, 16), 16)
            sums = list(sums)
            for j in range(FEAT // 128):
                cols = pl.ds(j * 128, 128)

                def read(q):
                    return CB[q, rows, cols].astype(F32) if q else OWN[rows, cols]

                own = read(p)
                for l in range(p + 1):
                    prod = own * read(l)
                    sums[l] = sums[l] + prod[:8] + prod[8:]
            return tuple(sums)

        sums = lax.fori_loop(0, 4, block, tuple(jnp.zeros((8, 128), F32) for _ in range(p + 1)))
        for l in range(p + 1):
            gram = put_pair(gram, pair(p), pair(l), sums[l])

    coef = tree_coefficients(sum_z(sum_plane(gram)), (1, 2))
    weights = [pick(coef, pair(p)) for p in range(4)]

    def final(i, carry):
        rows = pl.ds(pl.multiple_of(i * 16, 16), 16)
        near = weights[0] * OWN[rows, :] + weights[1] * CB[1, rows, :].astype(F32)
        far = weights[2] * CB[2, rows, :].astype(F32) + weights[3] * CB[3, rows, :].astype(F32)
        near_ref[rows, :] = near
        far_ref[rows, :] = far
        return carry

    lax.fori_loop(0, 4, final, 0)

    for cp in wcopies + xa + xb + xpair + [tpair] + tcopies[0] + tcopies[1] + list(ccopies.values()):
        cp.wait_send()


def on_device(inputs, weight, table, targets):
    vmem = pl.BlockSpec(memory_space=pltpu.VMEM)
    anywhere = pl.BlockSpec(memory_space=pl.ANY)
    dma = pltpu.SemaphoreType.DMA
    near, far = pl.pallas_call(
        kernel,
        out_shape=[jax.ShapeDtypeStruct((64, FEAT), F32)] * 2,
        in_specs=[anywhere, vmem, vmem, anywhere],
        out_specs=[vmem] * 2,
        scratch_shapes=[
            pltpu.VMEM((16, ROWS, FEAT), BF16),
            pltpu.VMEM((4, 64, FEAT), BF16),
            pltpu.VMEM((16, 8, 128), jnp.int32),
            pltpu.VMEM((4, 256, 128), BF16),
            pltpu.VMEM((256, HALF), BF16),
            pltpu.VMEM((8, 4, PIECE, HALF), F32),
            pltpu.VMEM((UNITS, 2, PIECE, 128), BF16),
            pltpu.VMEM((UNITS, 2, PIECE, HALF), BF16),
            pltpu.VMEM((UNITS, 2, PIECE, 128), BF16),
            pltpu.VMEM((UNITS, 2, PIECE, HALF), BF16),
            pltpu.VMEM((16, 4, PIECE, HALF), BF16),
            pltpu.VMEM((16, HALF, FEAT), F32),
            pltpu.VMEM((16, 128), F32),
            pltpu.VMEM((4, 64, FEAT), BF16),
            pltpu.VMEM((4, 64, FEAT), BF16),
            pltpu.VMEM((64, FEAT), F32),
            pltpu.VMEM((4, 16, 128), F32),
            pltpu.VMEM((16, 16, 128), F32),
            pltpu.VMEM((2, 8, 128), F32),
            pltpu.VMEM((16, 8, 128), F32),
            pltpu.VMEM((8, 8, 128), F32),
            dma((5,)),
            dma((4,)),
            dma((4,)),
            dma((2,)),
            dma((2,)),
            dma((2, 10)),
            dma((2, 10)),
            dma((2, 16)),
            dma((16,)),
            dma((4, 2, UNITS)),
            dma((4, 2, UNITS)),
            dma((4,)),
            dma((4,)),
            dma((5, 16)),
            dma((5, 16)),
        ],
        compiler_params=pltpu.CompilerParams(
            collective_id=0, has_side_effects=True, vmem_limit_bytes=56 * 1024 * 1024
        ),
    )(inputs, weight.T, targets[None], table)
    combined = near + far
    return combined.T, (weight.T - STEP * combined).T


def solution(mesh):
    split = Mesh(mesh.devices.reshape(8, 4, 2, mesh.shape["shard"]), AXES)
    return jax.shard_map(
        on_device,
        mesh=split,
        in_specs=(P(REP, "shard"), P("shard", REP), P(), P(REP + ("shard",))),
        out_specs=(P("shard", REP), P("shard", REP)),
        check_vma=False,
    )
```

```python
import functools

import jax
import jax.numpy as jnp
from jax import lax
from jax.experimental import pallas as pl
from jax.experimental.pallas import tpu as pltpu
from jax.sharding import Mesh
from jax.sharding import PartitionSpec as P

AXES = ("z", "x", "c", "shard")
REP = ("z", "x", "c")
MESH = pl.DeviceIdType.MESH
F32, BF16 = jnp.float32, jnp.bfloat16

EPS = 1e-06
STEP = 0.05

KX = (0, 0, -1, 1, -1, 1, 0, 0, 2, 2, -1, 1, -1, 1, 2, 2)
KC = (0, 1, 0, 0, 1, 1, 0, 1, 0, 1, 0, 0, 1, 1, 0, 1)
KM = (0, 0, 0, 0, 0, 0, 1, 1, 0, 0, 1, 1, 1, 1, 1, 1)
DZ = (0, 2, -2, 4)

ROWS, FEAT, PIECE, HALF = 320, 1024, 80, 256
UNITS, LAST = 16, 14


def place_of(steps, other, plane):
    return [i for i in range(16) if (KX[i] % 4, KC[i], KM[i]) == (steps % 4, other, plane)][0]


def block_of(steps):
    return [i for i in range(4) if DZ[i] % 8 == steps % 8][0]


def iotas(shape):
    return lax.broadcasted_iota(jnp.int32, shape, 0), lax.broadcasted_iota(jnp.int32, shape, 1)


def swap_bit(v, bit, axis):
    pos = lax.broadcasted_iota(jnp.int32, v.shape, axis)
    up = pltpu.roll(v, bit, axis)
    down = pltpu.roll(v, v.shape[axis] - bit, axis)
    return jnp.where((pos & bit) != 0, up, down)


def tree_coefficients(gram, bits):
    sub, lane = iotas(gram.shape)
    coef = jnp.ones((gram.shape[0], 1), F32)
    for bit in bits:
        own = jnp.where(lane == sub, gram, 0.0)
        cross = jnp.where(lane == (sub ^ bit), gram, 0.0)

        def factor(axis):
            norm = jnp.maximum(jnp.sum(own, axis=axis, keepdims=True), 0.0)
            return 1.0 - jnp.sum(cross, axis=axis, keepdims=True) / (2.0 * (norm + EPS))

        by_row, by_col = factor(1), factor(0)
        coef = coef * by_row
        gram = gram * by_row * by_col
        gram = gram + swap_bit(gram, bit, 1)
        gram = gram + swap_bit(gram, bit, 0)
    return coef


def pick(coef, index):
    sub, _ = iotas(coef.shape)
    return jnp.sum(jnp.where(sub == index, coef, 0.0), axis=0, keepdims=True)


def put_pair(gram, i, j, products):
    sub, lane = iotas(gram.shape)
    v = jnp.sum(jnp.sum(products, axis=0, keepdims=True), axis=1, keepdims=True)
    return jnp.where(((sub == i) & (lane == j)) | ((sub == j) & (lane == i)), v, gram)


def put_line(gram, i, others, products):
    sub, lane = iotas(gram.shape)
    lines = jnp.zeros(gram.shape, F32)
    for j, part in zip(others, products):
        lines = jnp.where(sub == j, jnp.sum(part, axis=0, keepdims=True), lines)
    column = jnp.sum(lines, axis=1, keepdims=True)
    row = jnp.sum(jnp.where(sub == lane, column, 0.0), axis=0, keepdims=True)
    return jnp.where(lane == i, column, jnp.where(sub == i, row, gram))


def kernel(
    x_ref, w_ref, tgt_ref, table_ref, near_ref, far_ref,
    X, W, TG, TB, TT, PF, S1, S2, R1, R2, E, G, GA, CS, CB, OWN, AC, AX, BC, BX, AZ,
    loc_sem, w_s, w_r, z_s, z_r, x_s, x_r, t_s, t_r, y_s, y_r, d_s, d_r, c_s, c_r, a_s, a_r,
):
    z, x = lax.axis_index("z"), lax.axis_index("x")
    c, y = lax.axis_index("c"), lax.axis_index("shard")

    def zat(d):
        return {"z": lax.rem(z + (d % 8), 8)}

    def yat(d):
        return {"shard": lax.rem(y + (d % 4), 4)}

    def xcat(d, o):
        dev = {}
        if d % 4:
            dev["x"] = lax.rem(x + (d % 4), 4)
        if o:
            dev["c"] = 1 - c
        return dev

    mine = lax.rem(z, 2)

    def partner(o):
        dev = {"z": z + 1 - 2 * mine}
        if o:
            dev["c"] = 1 - c
        return dev

    def xyat(d, e):
        return {"x": lax.rem(x + (d % 4), 4), "shard": lax.rem(y + (e % 4), 4)}

    def remote(src, dst, ssem, rsem, dev):
        return pltpu.make_async_remote_copy(
            src_ref=src, dst_ref=dst, send_sem=ssem, recv_sem=rsem, device_id=dev, device_id_type=MESH
        )

    barrier = pltpu.get_barrier_semaphore()
    others = [zat(d) for d in (4, 3, 5, 2, 6, 1, 7)]
    others += [xyat(d, e) for d in range(4) for e in range(4) if d or e]
    others += [xcat(d, 1) for d in range(4)] + [partner(1)]
    for dev in others:
        pl.semaphore_signal(barrier, inc=1, device_id=dev, device_id_type=MESH)
    TG[0] = jnp.zeros((8, 128), jnp.int32)
    TG[0, 0:1, 0:PIECE] = tgt_ref[...]

    own_x = pltpu.make_async_copy(x_ref, X.at[0], loc_sem.at[4])
    own_x.start()
    blocks = []
    for p in range(4):
        col = lax.rem(z + (DZ[p] % 8), 8) * 512 + x * 128
        cp = pltpu.make_async_copy(
            table_ref.at[:, pl.ds(pl.multiple_of(col, 128), 128)], TB.at[p], loc_sem.at[p]
        )
        cp.start()
        blocks.append(cp)

    W[0] = w_ref[...].astype(BF16)
    GA[...] = jnp.zeros_like(GA)

    for cp in blocks:
        cp.wait()
    _, lane = iotas((256, 128))
    for q in range(2):
        left = pltpu.roll(TB[2 * q].astype(F32), 64 * c, 1)
        right = pltpu.roll(TB[2 * q + 1].astype(F32), 64 * (1 - c), 1)
        TT[:, q * 128 : q * 128 + 128] = jnp.where(lane < 64, left, right).astype(BF16)

    own_x.wait()
    pl.semaphore_wait(barrier, len(others))

    def target_copy(k, m):
        there = place_of(-KX[k], KC[k], m)
        slot = place_of(0, 0, m)
        return remote(TG.at[slot], TG.at[there], t_s.at[m, k], t_r.at[there], xcat(KX[k], KC[k]))

    others_in_plane = [k for k in range(1, 16) if KM[k] == 0]
    tpair = remote(TG.at[0], TG.at[6], t_s.at[0, 0], t_r.at[6], partner(0))
    tcopies = [[target_copy(k, m) for k in others_in_plane] for m in range(2)]
    tpair.start()
    for tc in tcopies[0]:
        tc.start()

    upper, lower = pl.ds(0, 32), pl.ds(32, 32)
    plan = (
        (W.at[0], W.at[2], 2),
        (W.at[0], W.at[1], -2),
        (W.at[2, upper], W.at[3, upper], 2),
        (W.at[1, lower], W.at[3, lower], -2),
    )
    wcopies = [remote(a, b, w_s.at[i], w_r.at[i], zat(d)) for i, (a, b, d) in enumerate(plan)]
    wcopies[0].start()
    wcopies[1].start()

    lo, hi = pl.ds(0, 160), pl.ds(160, 160)
    xpair = [remote(X.at[0, h], X.at[6, h], z_s.at[i], z_r.at[i], partner(0)) for i, h in enumerate((lo, hi))]

    def around(m):
        own, core, left, right, far = (place_of(d, o, m) for d, o in ((0, 0), (0, 1), (-1, 0), (1, 0), (2, 0)))
        left_core, right_core, far_core = (place_of(d, 1, m) for d in (-1, 1, 2))
        plan = (
            (X.at[own, lo], X.at[left, lo], xcat(1, 0)),
            (X.at[own, hi], X.at[right, hi], xcat(-1, 0)),
            (X.at[own], X.at[core], xcat(0, 1)),
            (X.at[own, hi], X.at[left, hi], xcat(1, 0)),
            (X.at[own, lo], X.at[right, lo], xcat(-1, 0)),
            (X.at[left, lo], X.at[far, lo], xcat(1, 0)) if m == 0 else (X.at[8, lo], X.at[far, lo], partner(0)),
            (X.at[right, hi], X.at[far, hi], xcat(-1, 0)) if m == 0 else (X.at[8, hi], X.at[far, hi], partner(0)),
            (X.at[left], X.at[left_core], xcat(0, 1)),
            (X.at[right], X.at[right_core], xcat(0, 1)),
            (X.at[far], X.at[far_core], xcat(0, 1)),
        )
        return [remote(a, b, x_s.at[m, i], x_r.at[m, i], dev) for i, (a, b, dev) in enumerate(plan)]

    xa, xb = around(0), around(1)
    for i in range(5):
        xa[i].start()

    for i in (0, 1):
        wcopies[i].wait_recv()
        wcopies[i + 2].start()
    for cp in xpair:
        cp.start()
    tpair.wait_recv()
    for tc in tcopies[1]:
        tc.start()
    for i in (2, 3):
        wcopies[i].wait_recv()

    yp, ym, y2 = lax.rem(y + 1, 4), lax.rem(y + 3, 4), lax.rem(y + 2, 4)

    def r1(u, d):
        return remote(S1.at[u, d], R1.at[u, d], y_s.at[0, d, u], y_r.at[0, d, u], yat(1 - 2 * d))

    def r2(u, d):
        return remote(S2.at[u, d], R2.at[u, d], y_s.at[1, d, u], y_r.at[1, d, u], yat(1 - 2 * d))

    def a1(u, d, who):
        ref = E.at[u, who]
        return remote(ref, ref, y_s.at[2, d, u], y_r.at[2, d, u], yat(1 - 2 * d))

    def a3(u, who):
        ref = E.at[u, who]
        return remote(ref, ref, d_s.at[u - LAST], d_r.at[u - LAST], yat(2))

    def a2(u, d, who):
        ref = E.at[u, who, :, pl.ds(128 * d, 128)]
        return remote(ref, ref, y_s.at[3, d, u], y_r.at[3, d, u], yat(1 - 2 * d))

    def arrived(u):
        plan = {
            1: ((xa[2], None), (xa[0], xa[5]), (xa[1], xa[6])),
            2: ((xa[3], xa[7]),),
            3: ((xa[4], xa[8]),),
            4: ((xa[7], None), (xpair[0], xb[0], xb[4])),
            5: ((xa[8], None), (xpair[1], xb[1], xb[3], xb[2])),
            6: ((xa[5], xb[5]), (xa[6], xb[6], xa[9])),
            7: ((xb[2], None),),
            9: ((xa[9], None),),
            10: ((xb[0], None), (xb[3], xb[7])),
            11: ((xb[1], None), (xb[4], xb[8])),
            12: ((xb[7], None),),
            13: ((xb[8], None),),
            14: ((xb[5], None), (xb[6], xb[9])),
            15: ((xb[9], None),),
        }
        for turn, steps in plan.items():

            @pl.when(u == turn)
            def _(steps=steps):
                for first, *then in steps:
                    first.wait_recv()
                    for cp in then:
                        if cp is not None:
                            cp.start()

    def forward(u):
        slot = u % 8
        arrived(u)
        part = lax.dot_general(
            X[u], W[...].reshape(HALF, FEAT), (((1,), (1,)), ((), ())), preferred_element_type=F32
        )
        PF[slot] = part.reshape(4, PIECE, HALF)
        far = PF[slot, y2].astype(BF16)
        S1[u, 0] = far[:, :128]
        S1[u, 1] = far[:, 128:]
        r1(u, 0).start()
        r1(u, 1).start()

        @pl.when(u == 0)
        def _():
            for tc in tcopies[0]:
                tc.wait_recv()

        @pl.when(u == 6)
        def _():
            for tc in tcopies[1]:
                tc.wait_recv()

        row = TG[u][0:1]
        sub, _ = iotas((256, 128))
        one_hot = (sub == row).astype(F32).astype(BF16)
        wanted = lax.dot_general(one_hot, TT[...], (((0,), (0,)), ((), ())), preferred_element_type=F32)
        PF[slot, y] = PF[slot, y] - wanted[:PIECE]

    def reduce_step(u):
        slot = u % 8
        r1(u, 0).wait_recv()
        r1(u, 1).wait_recv()
        S2[u, 0, :, :128] = (PF[slot, yp, :, :128] + R1[u, 0].astype(F32)).astype(BF16)
        S2[u, 0, :, 128:] = PF[slot, yp, :, 128:].astype(BF16)
        r2(u, 0).start()
        S2[u, 1, :, :128] = PF[slot, ym, :, :128].astype(BF16)
        S2[u, 1, :, 128:] = (PF[slot, ym, :, 128:] + R1[u, 1].astype(F32)).astype(BF16)
        r2(u, 1).start()

    def error_step(u):
        slot = u % 8
        r2(u, 0).wait_recv()
        r2(u, 1).wait_recv()
        total = PF[slot, y] + R2[u, 0].astype(F32) + R2[u, 1].astype(F32)
        E[u, y] = (total * (1.0 / ROWS)).astype(BF16)
        a1(u, 0, y).start()
        a1(u, 1, y).start()

        @pl.when(u >= LAST)
        def _():
            a3(u, y).start()

    def spread_step(u):
        a1(u, 0, ym).wait_recv()
        a2(u, 0, ym).start()
        a1(u, 1, yp).wait_recv()
        a2(u, 1, yp).start()

    def replica(k):
        plane = lax.rem(mine + KM[k], 2)
        return plane * 8 + lax.rem(x + (KX[k] % 4), 4) * 2 + lax.rem(c + KC[k], 2)

    def grad_step(u):

        @pl.when(u < LAST)
        def _():
            a2(u, 0, y2).wait_recv()
            a2(u, 1, y2).wait_recv()

        @pl.when(u >= LAST)
        def _():
            a1(u, 0, ym).wait_recv()
            a1(u, 1, yp).wait_recv()
            a3(u, y2).wait_recv()

        err = E[u].reshape(ROWS, HALF)
        G[u] = lax.dot_general(err, X[u], (((0,), (0,)), ((), ())), preferred_element_type=F32)
        for kk in range(16):

            @pl.when(u == kk)
            def _():
                def block(i, sums):
                    rows = pl.ds(pl.multiple_of(i * 8, 8), 8)
                    sums = list(sums)
                    for j in range(FEAT // 128):
                        cols = pl.ds(j * 128, 128)
                        own = G[kk, rows, cols]
                        for l in range(kk):
                            sums[l] = sums[l] + own * G[l, rows, cols]
                        sums[kk] = sums[kk] + own * own
                    return tuple(sums)

                sums = lax.fori_loop(
                    0, HALF // 8, block, tuple(jnp.zeros((8, 128), F32) for _ in range(kk + 1))
                )
                GA[...] = put_line(GA[...], replica(kk), [replica(l) for l in range(kk + 1)], sums)

        for d in range(2):
            r2(u, d).wait_send()
            a1(u, d, y).wait_send()
            r1(u, d).wait_send()

        @pl.when(u < LAST)
        def _():
            a2(u, 0, ym).wait_send()
            a2(u, 1, yp).wait_send()

        @pl.when(u >= LAST)
        def _():
            a3(u, y).wait_send()

    def turn(t, carry):
        def at(u, low, high, step):
            @pl.when((u >= low) & (u < high))
            def _():
                step(u)

        at(t - 6, 0, LAST, spread_step)
        at(t - 4, 0, UNITS, error_step)
        at(t - 2, 0, UNITS, reduce_step)

        @pl.when(t < UNITS)
        def _():
            forward(t)

        at(t - 8, 0, UNITS, grad_step)
        return carry

    lax.fori_loop(0, UNITS + 8, turn, 0)

    def sum_xy(ref, s):
        copies = []
        for i in range(1, 16):
            d, e = i // 4, i % 4
            there = (-d) % 4 * 4 + (-e) % 4
            cp = remote(ref.at[0], ref.at[there], a_s.at[s, i], a_r.at[s, there], xyat(d, e))
            cp.start()
            copies.append(cp)
        for cp in copies:
            cp.wait()
        return jnp.sum(ref[...], axis=0)

    def sum_planes(value):
        AC[0] = value
        near = (xcat(0, 1), partner(0), partner(1))
        copies = [remote(AC.at[0], AC.at[i + 1], a_s.at[3, i], a_r.at[3, i], dev) for i, dev in enumerate(near)]
        for cp in copies:
            cp.start()
        for cp in copies:
            cp.wait()
        AX[0] = jnp.sum(AC[...], axis=0)
        return sum_xy(AX, 0)

    def sum_plane(value):
        BC[0] = value
        cp = remote(BC.at[0], BC.at[1], a_s.at[4, 0], a_r.at[4, 0], xcat(0, 1))
        cp.start()
        cp.wait()
        BX[0] = BC[0] + BC[1]
        return sum_xy(BX, 1)

    def sum_z(value):
        AZ[0] = value
        copies = []
        for d in range(1, 8):
            cp = remote(AZ.at[0], AZ.at[8 - d], a_s.at[2, d], a_r.at[2, 8 - d], zat(d))
            cp.start()
            copies.append(cp)
        for cp in copies:
            cp.wait()
        return functools.reduce(jnp.add, [AZ[k] for k in range(8)])

    coef = tree_coefficients(sum_planes(GA[...]), (1, 2, 4, 8))
    weights = [pick(coef, replica(k)) for k in range(16)]

    ccopies = {}
    for p in (3, 1, 2, 0):

        def mix(i, carry):
            rows = pl.ds(pl.multiple_of(p * 64 + i * 16, 16), 16)
            total = weights[0] * G[0, rows, :]
            for k in range(1, 16):
                total = total + weights[k] * G[k, rows, :]
            here = pl.ds(pl.multiple_of(i * 16, 16), 16)
            if p == 0:
                OWN[here, :] = total
            else:
                CS[p, here, :] = total.astype(BF16)
            return carry

        lax.fori_loop(0, 4, mix, 0)
        if p:
            there = block_of(-DZ[p])
            ccopies[there] = remote(CS.at[p], CB.at[there], c_s.at[p], c_r.at[there], zat(DZ[p]))
            ccopies[there].start()

    for cp in wcopies + xa + xb + xpair + [tpair] + tcopies[0] + tcopies[1]:
        cp.wait_send()

    def pair(p):
        return lax.rem(z + (DZ[p] % 8), 8) // 2

    gram = jnp.zeros((8, 128), F32)
    for p in range(4):
        if p:
            ccopies[p].wait_recv()

        def block(i, sums, p=p):
            rows = pl.ds(pl.multiple_of(i * 16, 16), 16)
            sums = list(sums)
            for j in range(FEAT // 128):
                cols = pl.ds(j * 128, 128)

                def read(q):
                    return CB[q, rows, cols].astype(F32) if q else OWN[rows, cols]

                own = read(p)
                for l in range(p + 1):
                    prod = own * read(l)
                    sums[l] = sums[l] + prod[:8] + prod[8:]
            return tuple(sums)

        sums = lax.fori_loop(0, 4, block, tuple(jnp.zeros((8, 128), F32) for _ in range(p + 1)))
        for l in range(p + 1):
            gram = put_pair(gram, pair(p), pair(l), sums[l])

    coef = tree_coefficients(sum_z(sum_plane(gram)), (1, 2))
    weights = [pick(coef, pair(p)) for p in range(4)]

    def final(i, carry):
        rows = pl.ds(pl.multiple_of(i * 16, 16), 16)
        near = weights[0] * OWN[rows, :] + weights[1] * CB[1, rows, :].astype(F32)
        far = weights[2] * CB[2, rows, :].astype(F32) + weights[3] * CB[3, rows, :].astype(F32)
        near_ref[rows, :] = near
        far_ref[rows, :] = far
        return carry

    lax.fori_loop(0, 4, final, 0)

    for cp in ccopies.values():
        cp.wait_send()


def on_device(inputs, weight, table, targets):
    vmem = pl.BlockSpec(memory_space=pltpu.VMEM)
    anywhere = pl.BlockSpec(memory_space=pl.ANY)
    dma = pltpu.SemaphoreType.DMA
    near, far = pl.pallas_call(
        kernel,
        out_shape=[jax.ShapeDtypeStruct((64, FEAT), F32)] * 2,
        in_specs=[anywhere, vmem, vmem, anywhere],
        out_specs=[vmem] * 2,
        scratch_shapes=[
            pltpu.VMEM((16, ROWS, FEAT), BF16),
            pltpu.VMEM((4, 64, FEAT), BF16),
            pltpu.VMEM((16, 8, 128), jnp.int32),
            pltpu.VMEM((4, 256, 128), BF16),
            pltpu.VMEM((256, HALF), BF16),
            pltpu.VMEM((8, 4, PIECE, HALF), F32),
            pltpu.VMEM((UNITS, 2, PIECE, 128), BF16),
            pltpu.VMEM((UNITS, 2, PIECE, HALF), BF16),
            pltpu.VMEM((UNITS, 2, PIECE, 128), BF16),
            pltpu.VMEM((UNITS, 2, PIECE, HALF), BF16),
            pltpu.VMEM((16, 4, PIECE, HALF), BF16),
            pltpu.VMEM((16, HALF, FEAT), F32),
            pltpu.VMEM((16, 128), F32),
            pltpu.VMEM((4, 64, FEAT), BF16),
            pltpu.VMEM((4, 64, FEAT), BF16),
            pltpu.VMEM((64, FEAT), F32),
            pltpu.VMEM((4, 16, 128), F32),
            pltpu.VMEM((16, 16, 128), F32),
            pltpu.VMEM((2, 8, 128), F32),
            pltpu.VMEM((16, 8, 128), F32),
            pltpu.VMEM((8, 8, 128), F32),
            dma((5,)),
            dma((4,)),
            dma((4,)),
            dma((2,)),
            dma((2,)),
            dma((2, 10)),
            dma((2, 10)),
            dma((2, 16)),
            dma((16,)),
            dma((4, 2, UNITS)),
            dma((4, 2, UNITS)),
            dma((UNITS - LAST,)),
            dma((UNITS - LAST,)),
            dma((4,)),
            dma((4,)),
            dma((5, 16)),
            dma((5, 16)),
        ],
        compiler_params=pltpu.CompilerParams(
            collective_id=0, has_side_effects=True, vmem_limit_bytes=56 * 1024 * 1024
        ),
    )(inputs, weight.T, targets[None], table)
    combined = near + far
    return combined.T, (weight.T - STEP * combined).T


def solution(mesh):
    split = Mesh(mesh.devices.reshape(8, 4, 2, mesh.shape["shard"]), AXES)
    return jax.shard_map(
        on_device,
        mesh=split,
        in_specs=(P(REP, "shard"), P("shard", REP), P(), P(REP + ("shard",))),
        out_specs=(P("shard", REP), P("shard", REP)),
        check_vma=False,
    )
```

```python
import functools

import jax
import jax.numpy as jnp
from jax import lax
from jax.experimental import pallas as pl
from jax.experimental.pallas import tpu as pltpu
from jax.sharding import Mesh
from jax.sharding import PartitionSpec as P

AXES = ("z", "x", "c", "shard")
REP = ("z", "x", "c")
MESH = pl.DeviceIdType.MESH
F32, BF16 = jnp.float32, jnp.bfloat16

EPS = 1e-06
STEP = 0.05

KX = (0, 0, -1, 1, -1, 1, 0, 0, 2, 2, -1, 1, -1, 1, 2, 2)
KC = (0, 1, 0, 0, 1, 1, 0, 1, 0, 1, 0, 0, 1, 1, 0, 1)
KM = (0, 0, 0, 0, 0, 0, 1, 1, 0, 0, 1, 1, 1, 1, 1, 1)
DZ = (0, 2, -2, 4)

ROWS, FEAT, PIECE, HALF = 320, 1024, 80, 256
UNITS, LAST = 16, 15


def place_of(steps, other, plane):
    return [i for i in range(16) if (KX[i] % 4, KC[i], KM[i]) == (steps % 4, other, plane)][0]


def block_of(steps):
    return [i for i in range(4) if DZ[i] % 8 == steps % 8][0]


def iotas(shape):
    return lax.broadcasted_iota(jnp.int32, shape, 0), lax.broadcasted_iota(jnp.int32, shape, 1)


def swap_bit(v, bit, axis):
    pos = lax.broadcasted_iota(jnp.int32, v.shape, axis)
    up = pltpu.roll(v, bit, axis)
    down = pltpu.roll(v, v.shape[axis] - bit, axis)
    return jnp.where((pos & bit) != 0, up, down)


def tree_coefficients(gram, bits):
    sub, lane = iotas(gram.shape)
    coef = jnp.ones((gram.shape[0], 1), F32)
    for bit in bits:
        own = jnp.where(lane == sub, gram, 0.0)
        cross = jnp.where(lane == (sub ^ bit), gram, 0.0)

        def factor(axis):
            norm = jnp.maximum(jnp.sum(own, axis=axis, keepdims=True), 0.0)
            return 1.0 - jnp.sum(cross, axis=axis, keepdims=True) / (2.0 * (norm + EPS))

        by_row, by_col = factor(1), factor(0)
        coef = coef * by_row
        gram = gram * by_row * by_col
        gram = gram + swap_bit(gram, bit, 1)
        gram = gram + swap_bit(gram, bit, 0)
    return coef


def pick(coef, index):
    sub, _ = iotas(coef.shape)
    return jnp.sum(jnp.where(sub == index, coef, 0.0), axis=0, keepdims=True)


def put_pair(gram, i, j, products):
    sub, lane = iotas(gram.shape)
    v = jnp.sum(jnp.sum(products, axis=0, keepdims=True), axis=1, keepdims=True)
    return jnp.where(((sub == i) & (lane == j)) | ((sub == j) & (lane == i)), v, gram)


def put_line(gram, i, others, products):
    sub, lane = iotas(gram.shape)
    lines = jnp.zeros(gram.shape, F32)
    for j, part in zip(others, products):
        lines = jnp.where(sub == j, jnp.sum(part, axis=0, keepdims=True), lines)
    column = jnp.sum(lines, axis=1, keepdims=True)
    row = jnp.sum(jnp.where(sub == lane, column, 0.0), axis=0, keepdims=True)
    return jnp.where(lane == i, column, jnp.where(sub == i, row, gram))


def kernel(
    x_ref, w_ref, tgt_ref, table_ref, near_ref, far_ref,
    X, W, TG, TB, TT, PF, S1, S2, R1, R2, E, G, GA, CS, CB, OWN, AC, AX, BC, BX, AZ,
    loc_sem, w_s, w_r, z_s, z_r, x_s, x_r, t_s, t_r, y_s, y_r, d_s, d_r, c_s, c_r, a_s, a_r,
):
    z, x = lax.axis_index("z"), lax.axis_index("x")
    c, y = lax.axis_index("c"), lax.axis_index("shard")

    def zat(d):
        return {"z": lax.rem(z + (d % 8), 8)}

    def yat(d):
        return {"shard": lax.rem(y + (d % 4), 4)}

    def xcat(d, o):
        dev = {}
        if d % 4:
            dev["x"] = lax.rem(x + (d % 4), 4)
        if o:
            dev["c"] = 1 - c
        return dev

    mine = lax.rem(z, 2)

    def partner(o):
        dev = {"z": z + 1 - 2 * mine}
        if o:
            dev["c"] = 1 - c
        return dev

    def xyat(d, e):
        return {"x": lax.rem(x + (d % 4), 4), "shard": lax.rem(y + (e % 4), 4)}

    def remote(src, dst, ssem, rsem, dev):
        return pltpu.make_async_remote_copy(
            src_ref=src, dst_ref=dst, send_sem=ssem, recv_sem=rsem, device_id=dev, device_id_type=MESH
        )

    barrier = pltpu.get_barrier_semaphore()
    others = [zat(d) for d in (4, 3, 5, 2, 6, 1, 7)]
    others += [xyat(d, e) for d in range(4) for e in range(4) if d or e]
    others += [xcat(d, 1) for d in range(4)] + [partner(1)]
    for dev in others:
        pl.semaphore_signal(barrier, inc=1, device_id=dev, device_id_type=MESH)
    TG[0] = jnp.zeros((8, 128), jnp.int32)
    TG[0, 0:1, 0:PIECE] = tgt_ref[...]

    own_x = pltpu.make_async_copy(x_ref, X.at[0], loc_sem.at[4])
    own_x.start()
    blocks = []
    for p in range(4):
        col = lax.rem(z + (DZ[p] % 8), 8) * 512 + x * 128
        cp = pltpu.make_async_copy(
            table_ref.at[:, pl.ds(pl.multiple_of(col, 128), 128)], TB.at[p], loc_sem.at[p]
        )
        cp.start()
        blocks.append(cp)

    W[0] = w_ref[...].astype(BF16)
    GA[...] = jnp.zeros_like(GA)

    for cp in blocks:
        cp.wait()
    _, lane = iotas((256, 128))
    for q in range(2):
        left = pltpu.roll(TB[2 * q].astype(F32), 64 * c, 1)
        right = pltpu.roll(TB[2 * q + 1].astype(F32), 64 * (1 - c), 1)
        TT[:, q * 128 : q * 128 + 128] = jnp.where(lane < 64, left, right).astype(BF16)

    own_x.wait()
    pl.semaphore_wait(barrier, len(others))

    def target_copy(k, m):
        there = place_of(-KX[k], KC[k], m)
        slot = place_of(0, 0, m)
        return remote(TG.at[slot], TG.at[there], t_s.at[m, k], t_r.at[there], xcat(KX[k], KC[k]))

    others_in_plane = [k for k in range(1, 16) if KM[k] == 0]
    tpair = remote(TG.at[0], TG.at[6], t_s.at[0, 0], t_r.at[6], partner(0))
    tcopies = [[target_copy(k, m) for k in others_in_plane] for m in range(2)]
    tpair.start()
    for tc in tcopies[0]:
        tc.start()

    upper, lower = pl.ds(0, 32), pl.ds(32, 32)
    plan = (
        (W.at[0], W.at[2], 2),
        (W.at[0], W.at[1], -2),
        (W.at[2, upper], W.at[3, upper], 2),
        (W.at[1, lower], W.at[3, lower], -2),
    )
    wcopies = [remote(a, b, w_s.at[i], w_r.at[i], zat(d)) for i, (a, b, d) in enumerate(plan)]
    wcopies[0].start()
    wcopies[1].start()

    lo, hi = pl.ds(0, 160), pl.ds(160, 160)
    xpair = [remote(X.at[0, h], X.at[6, h], z_s.at[i], z_r.at[i], partner(0)) for i, h in enumerate((lo, hi))]

    def around(m):
        own, core, left, right, far = (place_of(d, o, m) for d, o in ((0, 0), (0, 1), (-1, 0), (1, 0), (2, 0)))
        left_core, right_core, far_core = (place_of(d, 1, m) for d in (-1, 1, 2))
        plan = (
            (X.at[own, lo], X.at[left, lo], xcat(1, 0)),
            (X.at[own, hi], X.at[right, hi], xcat(-1, 0)),
            (X.at[own], X.at[core], xcat(0, 1)),
            (X.at[own, hi], X.at[left, hi], xcat(1, 0)),
            (X.at[own, lo], X.at[right, lo], xcat(-1, 0)),
            (X.at[left, lo], X.at[far, lo], xcat(1, 0)) if m == 0 else (X.at[8, lo], X.at[far, lo], partner(0)),
            (X.at[right, hi], X.at[far, hi], xcat(-1, 0)) if m == 0 else (X.at[8, hi], X.at[far, hi], partner(0)),
            (X.at[left], X.at[left_core], xcat(0, 1)),
            (X.at[right], X.at[right_core], xcat(0, 1)),
            (X.at[far], X.at[far_core], xcat(0, 1)),
        )
        return [remote(a, b, x_s.at[m, i], x_r.at[m, i], dev) for i, (a, b, dev) in enumerate(plan)]

    xa, xb = around(0), around(1)
    for i in range(5):
        xa[i].start()

    for i in (0, 1):
        wcopies[i].wait_recv()
        wcopies[i + 2].start()
    for cp in xpair:
        cp.start()
    tpair.wait_recv()
    for tc in tcopies[1]:
        tc.start()
    for i in (2, 3):
        wcopies[i].wait_recv()

    yp, ym, y2 = lax.rem(y + 1, 4), lax.rem(y + 3, 4), lax.rem(y + 2, 4)

    def r1(u, d):
        return remote(S1.at[u, d], R1.at[u, d], y_s.at[0, d, u], y_r.at[0, d, u], yat(1 - 2 * d))

    def r2(u, d):
        return remote(S2.at[u, d], R2.at[u, d], y_s.at[1, d, u], y_r.at[1, d, u], yat(1 - 2 * d))

    def a1(u, d, who):
        ref = E.at[u, who]
        return remote(ref, ref, y_s.at[2, d, u], y_r.at[2, d, u], yat(1 - 2 * d))

    def a3(u, who):
        ref = E.at[u, who]
        return remote(ref, ref, d_s.at[u - LAST], d_r.at[u - LAST], yat(2))

    def a2(u, d, who):
        ref = E.at[u, who, :, pl.ds(128 * d, 128)]
        return remote(ref, ref, y_s.at[3, d, u], y_r.at[3, d, u], yat(1 - 2 * d))

    def arrived(u):
        plan = {
            1: ((xa[2], None), (xa[0], xa[5]), (xa[1], xa[6])),
            2: ((xa[3], xa[7]),),
            3: ((xa[4], xa[8]),),
            4: ((xa[7], None),),
            5: ((xa[8], None), (xpair[0], xb[0], xb[4]),),
            6: ((xpair[1], xb[1], xb[3], xb[2]),),
            7: ((xb[2], None), (xa[5], xb[5]), (xa[6], xb[6], xa[9]),),
            9: ((xa[9], None),),
            10: ((xb[0], None), (xb[3], xb[7])),
            11: ((xb[1], None), (xb[4], xb[8])),
            12: ((xb[7], None),),
            13: ((xb[8], None),),
            14: ((xb[5], None), (xb[6], xb[9])),
            15: ((xb[9], None),),
        }
        for turn, steps in plan.items():

            @pl.when(u == turn)
            def _(steps=steps):
                for first, *then in steps:
                    first.wait_recv()
                    for cp in then:
                        if cp is not None:
                            cp.start()

    def forward(u):
        slot = u % 8
        arrived(u)
        part = lax.dot_general(
            X[u], W[...].reshape(HALF, FEAT), (((1,), (1,)), ((), ())), preferred_element_type=F32
        )
        PF[slot] = part.reshape(4, PIECE, HALF)
        far = PF[slot, y2].astype(BF16)
        S1[u, 0] = far[:, :128]
        S1[u, 1] = far[:, 128:]
        r1(u, 0).start()
        r1(u, 1).start()

        @pl.when(u == 0)
        def _():
            for tc in tcopies[0]:
                tc.wait_recv()

        @pl.when(u == 6)
        def _():
            for tc in tcopies[1]:
                tc.wait_recv()

        row = TG[u][0:1]
        sub, _ = iotas((256, 128))
        one_hot = (sub == row).astype(F32).astype(BF16)
        wanted = lax.dot_general(one_hot, TT[...], (((0,), (0,)), ((), ())), preferred_element_type=F32)
        PF[slot, y] = PF[slot, y] - wanted[:PIECE]

    def reduce_step(u):
        slot = u % 8
        r1(u, 0).wait_recv()
        r1(u, 1).wait_recv()
        S2[u, 0, :, :128] = (PF[slot, yp, :, :128] + R1[u, 0].astype(F32)).astype(BF16)
        S2[u, 0, :, 128:] = PF[slot, yp, :, 128:].astype(BF16)
        r2(u, 0).start()
        S2[u, 1, :, :128] = PF[slot, ym, :, :128].astype(BF16)
        S2[u, 1, :, 128:] = (PF[slot, ym, :, 128:] + R1[u, 1].astype(F32)).astype(BF16)
        r2(u, 1).start()

    def error_step(u):
        slot = u % 8
        r2(u, 0).wait_recv()
        r2(u, 1).wait_recv()
        total = PF[slot, y] + R2[u, 0].astype(F32) + R2[u, 1].astype(F32)
        E[u, y] = (total * (1.0 / ROWS)).astype(BF16)
        a1(u, 0, y).start()
        a1(u, 1, y).start()

        @pl.when(u >= LAST)
        def _():
            a3(u, y).start()

    def spread_step(u):
        a1(u, 0, ym).wait_recv()
        a2(u, 0, ym).start()
        a1(u, 1, yp).wait_recv()
        a2(u, 1, yp).start()

    def replica(k):
        plane = lax.rem(mine + KM[k], 2)
        return plane * 8 + lax.rem(x + (KX[k] % 4), 4) * 2 + lax.rem(c + KC[k], 2)

    def grad_step(u):

        @pl.when(u < LAST)
        def _():
            a2(u, 0, y2).wait_recv()
            a2(u, 1, y2).wait_recv()

        @pl.when(u >= LAST)
        def _():
            a1(u, 0, ym).wait_recv()
            a1(u, 1, yp).wait_recv()
            a3(u, y2).wait_recv()

        err = E[u].reshape(ROWS, HALF)
        G[u] = lax.dot_general(err, X[u], (((0,), (0,)), ((), ())), preferred_element_type=F32)
        for kk in range(16):

            @pl.when(u == kk)
            def _():
                def block(i, sums):
                    rows = pl.ds(pl.multiple_of(i * 8, 8), 8)
                    sums = list(sums)
                    for j in range(FEAT // 128):
                        cols = pl.ds(j * 128, 128)
                        own = G[kk, rows, cols]
                        for l in range(kk):
                            sums[l] = sums[l] + own * G[l, rows, cols]
                        sums[kk] = sums[kk] + own * own
                    return tuple(sums)

                sums = lax.fori_loop(
                    0, HALF // 8, block, tuple(jnp.zeros((8, 128), F32) for _ in range(kk + 1))
                )
                GA[...] = put_line(GA[...], replica(kk), [replica(l) for l in range(kk + 1)], sums)

        for d in range(2):
            r2(u, d).wait_send()
            a1(u, d, y).wait_send()
            r1(u, d).wait_send()

        @pl.when(u < LAST)
        def _():
            a2(u, 0, ym).wait_send()
            a2(u, 1, yp).wait_send()

        @pl.when(u >= LAST)
        def _():
            a3(u, y).wait_send()

    def turn(t, carry):
        def at(u, low, high, step):
            @pl.when((u >= low) & (u < high))
            def _():
                step(u)

        at(t - 6, 0, LAST, spread_step)
        at(t - 4, 0, UNITS, error_step)
        at(t - 2, 0, UNITS, reduce_step)
        at(t - 8, 0, UNITS, grad_step)
        @pl.when(t < UNITS)
        def _():
            forward(t)

        return carry

    lax.fori_loop(0, UNITS + 8, turn, 0)

    def sum_xy(ref, s):
        copies = []
        for i in range(1, 16):
            d, e = i // 4, i % 4
            there = (-d) % 4 * 4 + (-e) % 4
            cp = remote(ref.at[0], ref.at[there], a_s.at[s, i], a_r.at[s, there], xyat(d, e))
            cp.start()
            copies.append(cp)
        for cp in copies:
            cp.wait()
        return jnp.sum(ref[...], axis=0)

    def sum_planes(value):
        AC[0] = value
        near = (xcat(0, 1), partner(0), partner(1))
        copies = [remote(AC.at[0], AC.at[i + 1], a_s.at[3, i], a_r.at[3, i], dev) for i, dev in enumerate(near)]
        for cp in copies:
            cp.start()
        for cp in copies:
            cp.wait()
        AX[0] = jnp.sum(AC[...], axis=0)
        return sum_xy(AX, 0)

    def sum_plane(value):
        BC[0] = value
        cp = remote(BC.at[0], BC.at[1], a_s.at[4, 0], a_r.at[4, 0], xcat(0, 1))
        cp.start()
        cp.wait()
        BX[0] = BC[0] + BC[1]
        return sum_xy(BX, 1)

    def sum_z(value):
        AZ[0] = value
        copies = []
        for d in range(1, 8):
            cp = remote(AZ.at[0], AZ.at[8 - d], a_s.at[2, d], a_r.at[2, 8 - d], zat(d))
            cp.start()
            copies.append(cp)
        for cp in copies:
            cp.wait()
        return functools.reduce(jnp.add, [AZ[k] for k in range(8)])

    coef = tree_coefficients(sum_planes(GA[...]), (1, 2, 4, 8))
    weights = [pick(coef, replica(k)) for k in range(16)]

    ccopies = {}
    for p in (3, 1, 2, 0):

        def mix(i, carry):
            rows = pl.ds(pl.multiple_of(p * 64 + i * 16, 16), 16)
            total = weights[0] * G[0, rows, :]
            for k in range(1, 16):
                total = total + weights[k] * G[k, rows, :]
            here = pl.ds(pl.multiple_of(i * 16, 16), 16)
            if p == 0:
                OWN[here, :] = total
            else:
                CS[p, here, :] = total.astype(BF16)
            return carry

        lax.fori_loop(0, 4, mix, 0)
        if p:
            there = block_of(-DZ[p])
            ccopies[there] = remote(CS.at[p], CB.at[there], c_s.at[p], c_r.at[there], zat(DZ[p]))
            ccopies[there].start()

    for cp in wcopies + xa + xb + xpair + [tpair] + tcopies[0] + tcopies[1]:
        cp.wait_send()

    def pair(p):
        return lax.rem(z + (DZ[p] % 8), 8) // 2

    gram = jnp.zeros((8, 128), F32)
    for p in range(4):
        if p:
            ccopies[p].wait_recv()

        def block(i, sums, p=p):
            rows = pl.ds(pl.multiple_of(i * 16, 16), 16)
            sums = list(sums)
            for j in range(FEAT // 128):
                cols = pl.ds(j * 128, 128)

                def read(q):
                    return CB[q, rows, cols].astype(F32) if q else OWN[rows, cols]

                own = read(p)
                for l in range(p + 1):
                    prod = own * read(l)
                    sums[l] = sums[l] + prod[:8] + prod[8:]
            return tuple(sums)

        sums = lax.fori_loop(0, 4, block, tuple(jnp.zeros((8, 128), F32) for _ in range(p + 1)))
        for l in range(p + 1):
            gram = put_pair(gram, pair(p), pair(l), sums[l])

    coef = tree_coefficients(sum_z(sum_plane(gram)), (1, 2))
    weights = [pick(coef, pair(p)) for p in range(4)]

    def final(i, carry):
        rows = pl.ds(pl.multiple_of(i * 16, 16), 16)
        near = weights[0] * OWN[rows, :] + weights[1] * CB[1, rows, :].astype(F32)
        far = weights[2] * CB[2, rows, :].astype(F32) + weights[3] * CB[3, rows, :].astype(F32)
        near_ref[rows, :] = near
        far_ref[rows, :] = far
        return carry

    lax.fori_loop(0, 4, final, 0)

    for cp in ccopies.values():
        cp.wait_send()


def on_device(inputs, weight, table, targets):
    vmem = pl.BlockSpec(memory_space=pltpu.VMEM)
    anywhere = pl.BlockSpec(memory_space=pl.ANY)
    dma = pltpu.SemaphoreType.DMA
    near, far = pl.pallas_call(
        kernel,
        out_shape=[jax.ShapeDtypeStruct((64, FEAT), F32)] * 2,
        in_specs=[anywhere, vmem, vmem, anywhere],
        out_specs=[vmem] * 2,
        scratch_shapes=[
            pltpu.VMEM((16, ROWS, FEAT), BF16),
            pltpu.VMEM((4, 64, FEAT), BF16),
            pltpu.VMEM((16, 8, 128), jnp.int32),
            pltpu.VMEM((4, 256, 128), BF16),
            pltpu.VMEM((256, HALF), BF16),
            pltpu.VMEM((8, 4, PIECE, HALF), F32),
            pltpu.VMEM((UNITS, 2, PIECE, 128), BF16),
            pltpu.VMEM((UNITS, 2, PIECE, HALF), BF16),
            pltpu.VMEM((UNITS, 2, PIECE, 128), BF16),
            pltpu.VMEM((UNITS, 2, PIECE, HALF), BF16),
            pltpu.VMEM((16, 4, PIECE, HALF), BF16),
            pltpu.VMEM((16, HALF, FEAT), F32),
            pltpu.VMEM((16, 128), F32),
            pltpu.VMEM((4, 64, FEAT), BF16),
            pltpu.VMEM((4, 64, FEAT), BF16),
            pltpu.VMEM((64, FEAT), F32),
            pltpu.VMEM((4, 16, 128), F32),
            pltpu.VMEM((16, 16, 128), F32),
            pltpu.VMEM((2, 8, 128), F32),
            pltpu.VMEM((16, 8, 128), F32),
            pltpu.VMEM((8, 8, 128), F32),
            dma((5,)),
            dma((4,)),
            dma((4,)),
            dma((2,)),
            dma((2,)),
            dma((2, 10)),
            dma((2, 10)),
            dma((2, 16)),
            dma((16,)),
            dma((4, 2, UNITS)),
            dma((4, 2, UNITS)),
            dma((UNITS - LAST,)),
            dma((UNITS - LAST,)),
            dma((4,)),
            dma((4,)),
            dma((5, 16)),
            dma((5, 16)),
        ],
        compiler_params=pltpu.CompilerParams(
            collective_id=0, has_side_effects=True, vmem_limit_bytes=56 * 1024 * 1024
        ),
    )(inputs, weight.T, targets[None], table)
    combined = near + far
    return combined.T, (weight.T - STEP * combined).T


def solution(mesh):
    split = Mesh(mesh.devices.reshape(8, 4, 2, mesh.shape["shard"]), AXES)
    return jax.shard_map(
        on_device,
        mesh=split,
        in_specs=(P(REP, "shard"), P("shard", REP), P(), P(REP + ("shard",))),
        out_specs=(P("shard", REP), P("shard", REP)),
        check_vma=False,
    )
```

```python
import functools

import jax
import jax.numpy as jnp
from jax import lax
from jax.experimental import pallas as pl
from jax.experimental.pallas import tpu as pltpu
from jax.sharding import Mesh
from jax.sharding import PartitionSpec as P

AXES = ("z", "x", "c", "shard")
REP = ("z", "x", "c")
MESH = pl.DeviceIdType.MESH
F32, BF16 = jnp.float32, jnp.bfloat16

EPS = 1e-06
STEP = 0.05

KX = (0, 0, -1, 1, -1, 1, 0, 0, 2, 2, -1, 1, -1, 1, 2, 2)
KC = (0, 1, 0, 0, 1, 1, 0, 1, 0, 1, 0, 0, 1, 1, 0, 1)
KM = (0, 0, 0, 0, 0, 0, 1, 1, 0, 0, 1, 1, 1, 1, 1, 1)
DZ = (0, 2, -2, 4)

ROWS, FEAT, PIECE, HALF = 320, 1024, 80, 256
UNITS, LAST = 16, 15


def place_of(steps, other, plane):
    return [i for i in range(16) if (KX[i] % 4, KC[i], KM[i]) == (steps % 4, other, plane)][0]


def block_of(steps):
    return [i for i in range(4) if DZ[i] % 8 == steps % 8][0]


def iotas(shape):
    return lax.broadcasted_iota(jnp.int32, shape, 0), lax.broadcasted_iota(jnp.int32, shape, 1)


def swap_bit(v, bit, axis):
    pos = lax.broadcasted_iota(jnp.int32, v.shape, axis)
    up = pltpu.roll(v, bit, axis)
    down = pltpu.roll(v, v.shape[axis] - bit, axis)
    return jnp.where((pos & bit) != 0, up, down)


def tree_coefficients(gram, bits):
    sub, lane = iotas(gram.shape)
    coef = jnp.ones((gram.shape[0], 1), F32)
    for bit in bits:
        own = jnp.where(lane == sub, gram, 0.0)
        cross = jnp.where(lane == (sub ^ bit), gram, 0.0)

        def factor(axis):
            norm = jnp.maximum(jnp.sum(own, axis=axis, keepdims=True), 0.0)
            return 1.0 - jnp.sum(cross, axis=axis, keepdims=True) / (2.0 * (norm + EPS))

        by_row, by_col = factor(1), factor(0)
        coef = coef * by_row
        gram = gram * by_row * by_col
        gram = gram + swap_bit(gram, bit, 1)
        gram = gram + swap_bit(gram, bit, 0)
    return coef


def pick(coef, index):
    sub, _ = iotas(coef.shape)
    return jnp.sum(jnp.where(sub == index, coef, 0.0), axis=0, keepdims=True)


def put_pair(gram, i, j, products):
    sub, lane = iotas(gram.shape)
    v = jnp.sum(jnp.sum(products, axis=0, keepdims=True), axis=1, keepdims=True)
    return jnp.where(((sub == i) & (lane == j)) | ((sub == j) & (lane == i)), v, gram)


def put_line(gram, i, others, products):
    sub, lane = iotas(gram.shape)
    lines = jnp.zeros(gram.shape, F32)
    for j, part in zip(others, products):
        lines = jnp.where(sub == j, jnp.sum(part, axis=0, keepdims=True), lines)
    column = jnp.sum(lines, axis=1, keepdims=True)
    row = jnp.sum(jnp.where(sub == lane, column, 0.0), axis=0, keepdims=True)
    return jnp.where(lane == i, column, jnp.where(sub == i, row, gram))


def kernel(
    x_ref, w_ref, tgt_ref, table_ref, near_ref, far_ref,
    X, W, TG, TB, TT, PF, S1, S2, R1, R2, E, G, GA, CS, CB, OWN, AC, AX, BC, BX, AZ,
    loc_sem, w_s, w_r, z_s, z_r, x_s, x_r, t_s, t_r, y_s, y_r, d_s, d_r, c_s, c_r, a_s, a_r,
):
    z, x = lax.axis_index("z"), lax.axis_index("x")
    c, y = lax.axis_index("c"), lax.axis_index("shard")

    def zat(d):
        return {"z": lax.rem(z + (d % 8), 8)}

    def yat(d):
        return {"shard": lax.rem(y + (d % 4), 4)}

    def xcat(d, o):
        dev = {}
        if d % 4:
            dev["x"] = lax.rem(x + (d % 4), 4)
        if o:
            dev["c"] = 1 - c
        return dev

    mine = lax.rem(z, 2)

    def partner(o):
        dev = {"z": z + 1 - 2 * mine}
        if o:
            dev["c"] = 1 - c
        return dev

    def xyat(d, e):
        return {"x": lax.rem(x + (d % 4), 4), "shard": lax.rem(y + (e % 4), 4)}

    def remote(src, dst, ssem, rsem, dev):
        return pltpu.make_async_remote_copy(
            src_ref=src, dst_ref=dst, send_sem=ssem, recv_sem=rsem, device_id=dev, device_id_type=MESH
        )

    barrier = pltpu.get_barrier_semaphore()
    others = [zat(d) for d in (4, 3, 5, 2, 6, 1, 7)]
    others += [xyat(d, e) for d in range(4) for e in range(4) if d or e]
    others += [xcat(d, 1) for d in range(4)] + [partner(1)]
    for dev in others:
        pl.semaphore_signal(barrier, inc=1, device_id=dev, device_id_type=MESH)
    TG[0] = jnp.zeros((8, 128), jnp.int32)
    TG[0, 0:1, 0:PIECE] = tgt_ref[...]

    own_x = pltpu.make_async_copy(x_ref, X.at[0], loc_sem.at[4])
    own_x.start()
    blocks = []
    for p in range(4):
        col = lax.rem(z + (DZ[p] % 8), 8) * 512 + x * 128
        cp = pltpu.make_async_copy(
            table_ref.at[:, pl.ds(pl.multiple_of(col, 128), 128)], TB.at[p], loc_sem.at[p]
        )
        cp.start()
        blocks.append(cp)

    W[0] = w_ref[...].astype(BF16)
    GA[...] = jnp.zeros_like(GA)

    for cp in blocks:
        cp.wait()
    _, lane = iotas((256, 128))
    for q in range(2):
        left = pltpu.roll(TB[2 * q].astype(F32), 64 * c, 1)
        right = pltpu.roll(TB[2 * q + 1].astype(F32), 64 * (1 - c), 1)
        TT[:, q * 128 : q * 128 + 128] = jnp.where(lane < 64, left, right).astype(BF16)

    own_x.wait()
    pl.semaphore_wait(barrier, len(others))

    def target_copy(k, m):
        there = place_of(-KX[k], KC[k], m)
        slot = place_of(0, 0, m)
        return remote(TG.at[slot], TG.at[there], t_s.at[m, k], t_r.at[there], xcat(KX[k], KC[k]))

    others_in_plane = [k for k in range(1, 16) if KM[k] == 0]
    tpair = remote(TG.at[0], TG.at[6], t_s.at[0, 0], t_r.at[6], partner(0))
    tcopies = [[target_copy(k, m) for k in others_in_plane] for m in range(2)]
    tpair.start()
    for tc in tcopies[0]:
        tc.start()

    upper, lower = pl.ds(0, 32), pl.ds(32, 32)
    plan = (
        (W.at[0], W.at[2], 2),
        (W.at[0], W.at[1], -2),
        (W.at[2, upper], W.at[3, upper], 2),
        (W.at[1, lower], W.at[3, lower], -2),
    )
    wcopies = [remote(a, b, w_s.at[i], w_r.at[i], zat(d)) for i, (a, b, d) in enumerate(plan)]
    wcopies[0].start()
    wcopies[1].start()

    lo, hi = pl.ds(0, 160), pl.ds(160, 160)
    xpair = [remote(X.at[0, h], X.at[6, h], z_s.at[i], z_r.at[i], partner(0)) for i, h in enumerate((lo, hi))]

    def around(m):
        own, core, left, right, far = (place_of(d, o, m) for d, o in ((0, 0), (0, 1), (-1, 0), (1, 0), (2, 0)))
        left_core, right_core, far_core = (place_of(d, 1, m) for d in (-1, 1, 2))
        plan = (
            (X.at[own, lo], X.at[left, lo], xcat(1, 0)),
            (X.at[own, hi], X.at[right, hi], xcat(-1, 0)),
            (X.at[own], X.at[core], xcat(0, 1)),
            (X.at[own, hi], X.at[left, hi], xcat(1, 0)),
            (X.at[own, lo], X.at[right, lo], xcat(-1, 0)),
            (X.at[left, lo], X.at[far, lo], xcat(1, 0)) if m == 0 else (X.at[8, lo], X.at[far, lo], partner(0)),
            (X.at[right, hi], X.at[far, hi], xcat(-1, 0)) if m == 0 else (X.at[8, hi], X.at[far, hi], partner(0)),
            (X.at[left], X.at[left_core], xcat(0, 1)),
            (X.at[right], X.at[right_core], xcat(0, 1)),
            (X.at[far], X.at[far_core], xcat(0, 1)),
        )
        return [remote(a, b, x_s.at[m, i], x_r.at[m, i], dev) for i, (a, b, dev) in enumerate(plan)]

    xa, xb = around(0), around(1)
    for i in range(5):
        xa[i].start()

    for i in (0, 1):
        wcopies[i].wait_recv()
        wcopies[i + 2].start()
    for cp in xpair:
        cp.start()
    tpair.wait_recv()
    for tc in tcopies[1]:
        tc.start()
    for i in (2, 3):
        wcopies[i].wait_recv()

    yp, ym, y2 = lax.rem(y + 1, 4), lax.rem(y + 3, 4), lax.rem(y + 2, 4)

    def r1(u, d):
        return remote(S1.at[u, d], R1.at[u, d], y_s.at[0, d, u], y_r.at[0, d, u], yat(1 - 2 * d))

    def r2(u, d):
        return remote(S2.at[u, d], R2.at[u, d], y_s.at[1, d, u], y_r.at[1, d, u], yat(1 - 2 * d))

    def a1(u, d, who):
        ref = E.at[u, who]
        return remote(ref, ref, y_s.at[2, d, u], y_r.at[2, d, u], yat(1 - 2 * d))

    def a3(u, who):
        ref = E.at[u, who]
        return remote(ref, ref, d_s.at[u - LAST], d_r.at[u - LAST], yat(2))

    def a2(u, d, who):
        ref = E.at[u, who, :, pl.ds(128 * d, 128)]
        return remote(ref, ref, y_s.at[3, d, u], y_r.at[3, d, u], yat(1 - 2 * d))

    def arrived(u):
        plan = {
            1: ((xa[2], None), (xa[0], xa[5]), (xa[1], xa[6])),
            2: ((xa[3], xa[7]),),
            3: ((xa[4], xa[8]),),
            4: ((xa[7], None),),
            5: ((xa[8], None), (xpair[0], xb[0], xb[4]),),
            6: ((xpair[1], xb[1], xb[3], xb[2]),),
            7: ((xb[2], None), (xa[5], xb[5]), (xa[6], xb[6], xa[9]),),
            9: ((xa[9], None),),
            10: ((xb[0], None), (xb[3], xb[7])),
            11: ((xb[1], None), (xb[4], xb[8])),
            12: ((xb[7], None),),
            13: ((xb[8], None),),
            14: ((xb[5], None), (xb[6], xb[9])),
            15: ((xb[9], None),),
        }
        for turn, steps in plan.items():

            @pl.when(u == turn)
            def _(steps=steps):
                for first, *then in steps:
                    first.wait_recv()
                    for cp in then:
                        if cp is not None:
                            cp.start()

    def forward(u):
        slot = u % 8
        arrived(u)
        part = lax.dot_general(
            X[u], W[...].reshape(HALF, FEAT), (((1,), (1,)), ((), ())), preferred_element_type=F32
        )
        PF[slot] = part.reshape(4, PIECE, HALF)
        far = PF[slot, y2].astype(BF16)
        S1[u, 0] = far[:, :128]
        S1[u, 1] = far[:, 128:]
        r1(u, 0).start()
        r1(u, 1).start()

        @pl.when(u == 0)
        def _():
            for tc in tcopies[0]:
                tc.wait_recv()

        @pl.when(u == 6)
        def _():
            for tc in tcopies[1]:
                tc.wait_recv()

        row = TG[u][0:1]
        sub, _ = iotas((256, 128))
        one_hot = (sub == row).astype(F32).astype(BF16)
        wanted = lax.dot_general(one_hot, TT[...], (((0,), (0,)), ((), ())), preferred_element_type=F32)
        PF[slot, y] = PF[slot, y] - wanted[:PIECE]

    def reduce_step(u):
        slot = u % 8
        r1(u, 0).wait_recv()
        r1(u, 1).wait_recv()
        S2[u, 0, :, :128] = (PF[slot, yp, :, :128] + R1[u, 0].astype(F32)).astype(BF16)
        S2[u, 0, :, 128:] = PF[slot, yp, :, 128:].astype(BF16)
        r2(u, 0).start()
        S2[u, 1, :, :128] = PF[slot, ym, :, :128].astype(BF16)
        S2[u, 1, :, 128:] = (PF[slot, ym, :, 128:] + R1[u, 1].astype(F32)).astype(BF16)
        r2(u, 1).start()

    def error_step(u):
        slot = u % 8
        r2(u, 0).wait_recv()
        r2(u, 1).wait_recv()
        total = PF[slot, y] + R2[u, 0].astype(F32) + R2[u, 1].astype(F32)
        E[u, y] = (total * (1.0 / ROWS)).astype(BF16)
        a1(u, 0, y).start()
        a1(u, 1, y).start()

        @pl.when(u >= LAST)
        def _():
            a3(u, y).start()

    def spread_step(u):
        a1(u, 0, ym).wait_recv()
        a2(u, 0, ym).start()
        a1(u, 1, yp).wait_recv()
        a2(u, 1, yp).start()

    def replica(k):
        plane = lax.rem(mine + KM[k], 2)
        return plane * 8 + lax.rem(x + (KX[k] % 4), 4) * 2 + lax.rem(c + KC[k], 2)

    def grad_step(u):

        @pl.when(u < LAST)
        def _():
            a2(u, 0, y2).wait_recv()
            a2(u, 1, y2).wait_recv()

        @pl.when(u >= LAST)
        def _():
            a1(u, 0, ym).wait_recv()
            a1(u, 1, yp).wait_recv()
            a3(u, y2).wait_recv()

        err = E[u].reshape(ROWS, HALF)
        G[u] = lax.dot_general(err, X[u], (((0,), (0,)), ((), ())), preferred_element_type=F32)
        for kk in range(16):

            @pl.when(u == kk)
            def _():
                def block(i, sums):
                    rows = pl.ds(pl.multiple_of(i * 8, 8), 8)
                    sums = list(sums)
                    for j in range(FEAT // 128):
                        cols = pl.ds(j * 128, 128)
                        own = G[kk, rows, cols]
                        for l in range(kk):
                            sums[l] = sums[l] + own * G[l, rows, cols]
                        sums[kk] = sums[kk] + own * own
                    return tuple(sums)

                sums = lax.fori_loop(
                    0, HALF // 8, block, tuple(jnp.zeros((8, 128), F32) for _ in range(kk + 1))
                )
                GA[...] = put_line(GA[...], replica(kk), [replica(l) for l in range(kk + 1)], sums)

        for d in range(2):
            r2(u, d).wait_send()
            a1(u, d, y).wait_send()
            r1(u, d).wait_send()

        @pl.when(u < LAST)
        def _():
            a2(u, 0, ym).wait_send()
            a2(u, 1, yp).wait_send()

        @pl.when(u >= LAST)
        def _():
            a3(u, y).wait_send()

    def turn(t, carry):
        def at(u, low, high, step):
            @pl.when((u >= low) & (u < high))
            def _():
                step(u)

        at(t - 6, 0, LAST, spread_step)
        at(t - 4, 0, UNITS, error_step)
        at(t - 2, 0, UNITS, reduce_step)
        at(t - 8, 0, UNITS, grad_step)
        @pl.when(t < UNITS)
        def _():
            forward(t)

        return carry

    lax.fori_loop(0, UNITS + 8, turn, 0)

    def sum_xy(ref, s):
        copies = []
        for i in (10, 6, 14, 9, 11, 2, 8, 5, 7, 13, 15, 1, 3, 4, 12):
            d, e = i // 4, i % 4
            there = (-d) % 4 * 4 + (-e) % 4
            cp = remote(ref.at[0], ref.at[there], a_s.at[s, i], a_r.at[s, there], xyat(d, e))
            cp.start()
            copies.append(cp)
        for cp in copies:
            cp.wait()
        return jnp.sum(ref[...], axis=0)

    def sum_planes(value):
        AC[0] = value
        near = (xcat(0, 1), partner(0), partner(1))
        copies = [remote(AC.at[0], AC.at[i + 1], a_s.at[3, i], a_r.at[3, i], dev) for i, dev in enumerate(near)]
        for cp in copies:
            cp.start()
        for cp in copies:
            cp.wait()
        AX[0] = jnp.sum(AC[...], axis=0)
        return sum_xy(AX, 0)

    def sum_plane(value):
        BC[0] = value
        cp = remote(BC.at[0], BC.at[1], a_s.at[4, 0], a_r.at[4, 0], xcat(0, 1))
        cp.start()
        cp.wait()
        BX[0] = BC[0] + BC[1]
        return sum_xy(BX, 1)

    def sum_z(value):
        AZ[0] = value
        copies = []
        for d in (4, 3, 5, 2, 6, 1, 7):
            cp = remote(AZ.at[0], AZ.at[8 - d], a_s.at[2, d], a_r.at[2, 8 - d], zat(d))
            cp.start()
            copies.append(cp)
        for cp in copies:
            cp.wait()
        return functools.reduce(jnp.add, [AZ[k] for k in range(8)])

    coef = tree_coefficients(sum_planes(GA[...]), (1, 2, 4, 8))
    weights = [pick(coef, replica(k)) for k in range(16)]

    ccopies = {}
    for p in (3, 1, 2, 0):

        def mix(i, carry):
            rows = pl.ds(pl.multiple_of(p * 64 + i * 16, 16), 16)
            total = weights[0] * G[0, rows, :]
            for k in range(1, 16):
                total = total + weights[k] * G[k, rows, :]
            here = pl.ds(pl.multiple_of(i * 16, 16), 16)
            if p == 0:
                OWN[here, :] = total
            else:
                CS[p, here, :] = total.astype(BF16)
            return carry

        lax.fori_loop(0, 4, mix, 0)
        if p:
            there = block_of(-DZ[p])
            ccopies[there] = remote(CS.at[p], CB.at[there], c_s.at[p], c_r.at[there], zat(DZ[p]))
            ccopies[there].start()

    for cp in wcopies + xa + xb + xpair + [tpair] + tcopies[0] + tcopies[1]:
        cp.wait_send()

    def pair(p):
        return lax.rem(z + (DZ[p] % 8), 8) // 2

    gram = jnp.zeros((8, 128), F32)
    for p in range(4):
        if p:
            ccopies[p].wait_recv()

        def block(i, sums, p=p):
            rows = pl.ds(pl.multiple_of(i * 16, 16), 16)
            sums = list(sums)
            for j in range(FEAT // 128):
                cols = pl.ds(j * 128, 128)

                def read(q):
                    return CB[q, rows, cols].astype(F32) if q else OWN[rows, cols]

                own = read(p)
                for l in range(p + 1):
                    prod = own * read(l)
                    sums[l] = sums[l] + prod[:8] + prod[8:]
            return tuple(sums)

        sums = lax.fori_loop(0, 4, block, tuple(jnp.zeros((8, 128), F32) for _ in range(p + 1)))
        for l in range(p + 1):
            gram = put_pair(gram, pair(p), pair(l), sums[l])

    coef = tree_coefficients(sum_z(sum_plane(gram)), (1, 2))
    weights = [pick(coef, pair(p)) for p in range(4)]

    def final(i, carry):
        rows = pl.ds(pl.multiple_of(i * 16, 16), 16)
        near = weights[0] * OWN[rows, :] + weights[1] * CB[1, rows, :].astype(F32)
        far = weights[2] * CB[2, rows, :].astype(F32) + weights[3] * CB[3, rows, :].astype(F32)
        near_ref[rows, :] = near
        far_ref[rows, :] = far
        return carry

    lax.fori_loop(0, 4, final, 0)

    for cp in ccopies.values():
        cp.wait_send()


def on_device(inputs, weight, table, targets):
    vmem = pl.BlockSpec(memory_space=pltpu.VMEM)
    anywhere = pl.BlockSpec(memory_space=pl.ANY)
    dma = pltpu.SemaphoreType.DMA
    near, far = pl.pallas_call(
        kernel,
        out_shape=[jax.ShapeDtypeStruct((64, FEAT), F32)] * 2,
        in_specs=[anywhere, vmem, vmem, anywhere],
        out_specs=[vmem] * 2,
        scratch_shapes=[
            pltpu.VMEM((16, ROWS, FEAT), BF16),
            pltpu.VMEM((4, 64, FEAT), BF16),
            pltpu.VMEM((16, 8, 128), jnp.int32),
            pltpu.VMEM((4, 256, 128), BF16),
            pltpu.VMEM((256, HALF), BF16),
            pltpu.VMEM((8, 4, PIECE, HALF), F32),
            pltpu.VMEM((UNITS, 2, PIECE, 128), BF16),
            pltpu.VMEM((UNITS, 2, PIECE, HALF), BF16),
            pltpu.VMEM((UNITS, 2, PIECE, 128), BF16),
            pltpu.VMEM((UNITS, 2, PIECE, HALF), BF16),
            pltpu.VMEM((16, 4, PIECE, HALF), BF16),
            pltpu.VMEM((16, HALF, FEAT), F32),
            pltpu.VMEM((16, 128), F32),
            pltpu.VMEM((4, 64, FEAT), BF16),
            pltpu.VMEM((4, 64, FEAT), BF16),
            pltpu.VMEM((64, FEAT), F32),
            pltpu.VMEM((4, 16, 128), F32),
            pltpu.VMEM((16, 16, 128), F32),
            pltpu.VMEM((2, 8, 128), F32),
            pltpu.VMEM((16, 8, 128), F32),
            pltpu.VMEM((8, 8, 128), F32),
            dma((5,)),
            dma((4,)),
            dma((4,)),
            dma((2,)),
            dma((2,)),
            dma((2, 10)),
            dma((2, 10)),
            dma((2, 16)),
            dma((16,)),
            dma((4, 2, UNITS)),
            dma((4, 2, UNITS)),
            dma((UNITS - LAST,)),
            dma((UNITS - LAST,)),
            dma((4,)),
            dma((4,)),
            dma((5, 16)),
            dma((5, 16)),
        ],
        compiler_params=pltpu.CompilerParams(
            collective_id=0, has_side_effects=True, vmem_limit_bytes=56 * 1024 * 1024
        ),
    )(inputs, weight.T, targets[None], table)
    combined = near + far
    return combined.T, (weight.T - STEP * combined).T


def solution(mesh):
    split = Mesh(mesh.devices.reshape(8, 4, 2, mesh.shape["shard"]), AXES)
    return jax.shard_map(
        on_device,
        mesh=split,
        in_specs=(P(REP, "shard"), P("shard", REP), P(), P(REP + ("shard",))),
        out_specs=(P("shard", REP), P("shard", REP)),
        check_vma=False,
    )
```
